128 devices in a mesh: dp: 8 (over y, core), ctx: 16 (over z, x).
Axes of the slice: x: 4, y: 4, z: 4, core: 2. Of those that a mesh axis runs over, the one named last changes fastest.
Arguments:
- query: bfloat16 [8, 2048, 4096], P('dp', 'ctx'), may hold values from -140 to 140
- key_states: bfloat16 [8, 2048, 4096], P('dp', 'ctx'), may hold values from -7 to 7
- value_states: bfloat16 [8, 2048, 4096], P('dp', 'ctx'), may hold values from -6 to 6
- block_out: bfloat16 [8, 2048, 5120], P('dp', 'ctx'), may hold values from -6 to 6
- gate_mod: float32 [8, 5120], P('dp'), may hold values from 0.3 to 1.5
- head_mod: float32 [8, 2, 5120], P('dp'), may hold values from -4 to 4
- head_weight: bfloat16 [64, 5120], replicated, may hold values from -0.078125 to 0.078125
- proj_weight: bfloat16 [4096, 5120], P('ctx', 'dp'), may hold values from -0.09375 to 0.09375
- uncond_pred: float32 [8, 2048, 64], P('dp', 'ctx'), may hold values from -18 to 18
- target: float32 [8, 2048, 64], P('dp', 'ctx'), may hold values from -6 to 6
Outputs:
- grad_query: bfloat16 [8, 2048, 4096], P('dp', 'ctx')
- grad_key: bfloat16 [8, 2048, 4096], P('dp', 'ctx')
- grad_value: bfloat16 [8, 2048, 4096], P('dp', 'ctx')
- grad_stream: bfloat16 [8, 2048, 5120], P('dp', 'ctx')
- grad_proj: float32 [4096, 5120], P('ctx', 'dp')
- sample_loss: float32 [8], P('dp')
The draws below stay inside these ranges and needn't reach their ends.
All inputs are finite; a program needn't handle non-finite values.
Results may differ from the reference program's by a relative error of at most 0.017.
Values may be sent and summed in bfloat16 or wider, within the bound.
A program may use at most 256 MiB of HBM per device.

```python
import math
import jax
import jax.numpy as jnp
from jax import lax

D = 5120
HD = 128
PATCH = 64
HEADS = 32
SEQ = 2048
SAMPLES = 8


def shared_rows(key):
    return jnp.clip(jax.random.normal(key, (SAMPLES, SEQ, HEADS * HD), jnp.float32), -6.0, 6.0)


def draw_query(key, part):
    shared = shared_rows(key)
    key = jax.random.fold_in(key, 5)
    fresh_rows = jnp.clip(jax.random.normal(key, shared.shape, jnp.float32), -6.0, 6.0)
    return fresh_rows.astype(jnp.bfloat16)


def draw_key_states(key, part):
    shared = shared_rows(key)
    return shared.astype(jnp.bfloat16)


def draw_uncond_pred(key, part):
    key = jax.random.fold_in(key, 13)
    position = jnp.arange(SEQ).astype(jnp.float32)[None, :, None]
    rising = 1.0 + 2.0 * position / SEQ
    noise = jnp.clip(jax.random.normal(key, (SAMPLES, SEQ, PATCH), jnp.float32), -6.0, 6.0)
    return noise * rising


def shard_levels(own_key, extent, pieces, least, high):
    level = 1.0
    for dim, parts in pieces:
        heights = jax.random.uniform(jax.random.fold_in(jax.random.fold_in(own_key, 6), dim), (parts,), jnp.float32, least / len(pieces), high / len(pieces))
        level = level * jnp.repeat(jnp.exp(heights), extent[dim] // parts).reshape((-1,) + (1,) * (len(extent) - 1 - dim))
    return level


def bell_draw(key, shape, scale, bound, shards=(), held_as=jnp.bfloat16):
    loudness = shard_levels(key, shape, shards, -0.22, 0.18) if shards else 1.0
    drawn = jax.random.normal(key, shape, jnp.float32) * scale * loudness
    return jnp.minimum(jnp.maximum(drawn, -bound), bound).astype(held_as)


def setup_inputs(seed: int = 0) -> dict:
    key_list = jax.random.split(jax.random.key(seed), 11)
    query = draw_query(jax.random.fold_in(key_list[10], 71), 0)
    key_states = draw_key_states(jax.random.fold_in(key_list[10], 71), 0)
    value_states = bell_draw(key_list[2], (SAMPLES, SEQ, HEADS * HD), 1.0, 6.0, ((0, 8), (1, 16)))
    block_out = bell_draw(key_list[3], (SAMPLES, SEQ, D), 1.0, 6.0, ((0, 8), (1, 16)))
    gate_mod = jnp.clip(0.3 + 1.2 * jax.random.uniform(key_list[4], (SAMPLES, D), jnp.float32) ** shard_levels(key_list[4], (SAMPLES, D), ((0, 8),), -0.2, 0.2), 0.3, 1.5)
    head_mod = bell_draw(key_list[5], (SAMPLES, 2, D), 0.3, 4.0, ((0, 8),), jnp.float32)
    head_weight = bell_draw(key_list[6], (PATCH, D), D ** -0.5, 0.078125)
    proj_weight = bell_draw(key_list[7], (HEADS * HD, D), (HEADS * HD) ** -0.5, 0.09375, ((0, 16), (1, 8)))
    uncond_pred = draw_uncond_pred(jax.random.fold_in(key_list[10], 71), 0)
    target = bell_draw(key_list[9], (SAMPLES, SEQ, PATCH), 2.0, 6.0, ((0, 8), (1, 16)), jnp.float32)
    return dict(query=query, key_states=key_states, value_states=value_states, block_out=block_out, gate_mod=gate_mod, head_mod=head_mod, head_weight=head_weight, proj_weight=proj_weight, uncond_pred=uncond_pred, target=target)


guidance = 5.0
rescale_mix = 0.7
norm_epsilon = 1e-06
spread_epsilon = 1e-05

def sigma_of(first_sum, square_sum, cell_count):
    mean_value = first_sum / cell_count
    return jnp.sqrt(square_sum / cell_count - mean_value * mean_value + spread_epsilon)

def head_backward(operands):
    query_rows, key_rows, value_rows, out_grad = operands
    factor = 1.0 / math.sqrt(query_rows.shape[-1])
    scores = jnp.dot(query_rows, key_rows.T, preferred_element_type=jnp.float32) * factor
    attn_probs = jax.nn.softmax(scores, axis=-1)
    probs_low = attn_probs.astype(jnp.bfloat16)
    attended = jnp.dot(probs_low, value_rows, preferred_element_type=jnp.float32).astype(jnp.bfloat16)
    value_grad = jnp.dot(probs_low.T, out_grad, preferred_element_type=jnp.float32).astype(jnp.bfloat16)
    prob_grad = jnp.dot(out_grad, value_rows.T, preferred_element_type=jnp.float32)
    row_delta = lax.optimization_barrier(jnp.sum(attn_probs * prob_grad, axis=-1, keepdims=True))
    score_grad = (attn_probs * (prob_grad - row_delta) * factor).astype(jnp.bfloat16)
    query_grad = jnp.dot(score_grad, key_rows, preferred_element_type=jnp.float32).astype(jnp.bfloat16)
    key_grad = jnp.dot(score_grad.T, query_rows, preferred_element_type=jnp.float32).astype(jnp.bfloat16)
    return (attended, query_grad, key_grad, value_grad)

def reference(query, key_states, value_states, block_out, gate_mod, head_mod, head_weight, proj_weight, uncond_pred, target):
    cell_count = SEQ * PATCH
    highest = lax.Precision.HIGHEST
    values = block_out.astype(jnp.float32)
    center = lax.optimization_barrier(jnp.mean(values, axis=-1, keepdims=True))
    spread = lax.optimization_barrier(jnp.mean(jnp.square(values - center), axis=-1, keepdims=True))
    inverse = lax.rsqrt(spread + norm_epsilon)
    normed = (values - center) * inverse
    shift_rows = head_mod[:, 0][:, None, :]
    scale_rows = head_mod[:, 1][:, None, :]
    hidden = (normed * (1.0 + scale_rows) + shift_rows).astype(jnp.bfloat16)
    cond_pred = jnp.einsum('std,pd->stp', hidden.astype(jnp.float32), head_weight.astype(jnp.float32), precision=highest)
    guided = uncond_pred + guidance * (cond_pred - uncond_pred)
    sum_cond = lax.optimization_barrier(jnp.sum(cond_pred, axis=(1, 2)))
    sigma_cond = sigma_of(sum_cond, lax.optimization_barrier(jnp.sum(cond_pred * cond_pred, axis=(1, 2))), cell_count)
    sum_guided = lax.optimization_barrier(jnp.sum(guided, axis=(1, 2)))
    sigma_guided = sigma_of(sum_guided, lax.optimization_barrier(jnp.sum(guided * guided, axis=(1, 2))), cell_count)
    mix_ratio = rescale_mix * sigma_cond / sigma_guided + (1.0 - rescale_mix)
    final = mix_ratio[:, None, None] * guided
    sample_loss = lax.optimization_barrier(jnp.mean(jnp.square(final - target), axis=(1, 2)))
    final_grad = 2.0 * (final - target)
    slope_sum = lax.optimization_barrier(jnp.sum(final_grad * guided, axis=(1, 2)))
    mean_guided = (sum_guided / cell_count)[:, None, None]
    mean_cond = (sum_cond / cell_count)[:, None, None]
    guided_coef = (slope_sum * rescale_mix * sigma_cond / (cell_count * sigma_guided ** 3))[:, None, None]
    guided_grad = mix_ratio[:, None, None] * final_grad - guided_coef * (guided - mean_guided)
    cond_coef = (slope_sum * rescale_mix / (cell_count * sigma_guided * sigma_cond))[:, None, None]
    cond_grad = (guidance * guided_grad + cond_coef * (cond_pred - mean_cond)).astype(jnp.bfloat16)
    head_grad = jnp.einsum('stp,pd->std', cond_grad.astype(jnp.float32), head_weight.astype(jnp.float32), precision=highest) * (1.0 + scale_rows)
    mean_one = lax.optimization_barrier(jnp.mean(head_grad, axis=-1, keepdims=True))
    mean_two = lax.optimization_barrier(jnp.mean(head_grad * normed, axis=-1, keepdims=True))
    stream_grad = (head_grad - mean_one - normed * mean_two) * inverse
    grad_stream = stream_grad.astype(jnp.bfloat16)
    proj_input = (gate_mod[:, None, :] * stream_grad).astype(jnp.bfloat16)
    attn_grad = jnp.einsum('std,fd->stf', proj_input.astype(jnp.float32), proj_weight.astype(jnp.float32), precision=highest).astype(jnp.bfloat16)
    samples, seq_len, features = query.shape
    head_count = features // HD

    def split_heads(array):
        return array.reshape(samples, seq_len, head_count, HD).transpose(0, 2, 1, 3).reshape(samples * head_count, seq_len, HD)

    def join_heads(array):
        return array.reshape(samples, head_count, seq_len, HD).transpose(0, 2, 1, 3).reshape(samples, seq_len, features)
    attended, query_grad, key_grad, value_grad = lax.map(head_backward, (split_heads(query), split_heads(key_states), split_heads(value_states), split_heads(attn_grad)))
    attended = join_heads(attended)
    grad_proj = jnp.einsum('stf,std->fd', attended.astype(jnp.float32), proj_input.astype(jnp.float32), precision=highest)
    return (join_heads(query_grad), join_heads(key_grad), join_heads(value_grad), grad_stream, grad_proj, sample_loss)
```

```python
import functools

import jax
import jax.numpy as jnp
from jax import lax
from jax.experimental import pallas as pl
from jax.experimental.pallas import tpu as pltpu
from jax.sharding import PartitionSpec as P

HD = 128
PAIR = 2 * HD
SHARDS = 16
SCALE = 1.0 / float(HD) ** 0.5
EXP2_SCALE = 1.4426950408889634 * SCALE
MESH = pl.DeviceIdType.MESH

guidance = 5.0
rescale_mix = 0.7
norm_epsilon = 1e-06
spread_epsilon = 1e-05


def dot_nt(left, right):
    return lax.dot_general(left, right, (((1,), (1,)), ((), ())), preferred_element_type=jnp.float32)


def dot_nn(left, right):
    return lax.dot_general(left, right, (((1,), (0,)), ((), ())), preferred_element_type=jnp.float32)


def sigma_of(first_sum, square_sum, cell_count):
    mean_value = first_sum / cell_count
    return jnp.sqrt(square_sum / cell_count - mean_value * mean_value + spread_epsilon)


class Place:
    def __init__(self):
        dp = lax.axis_index("dp")
        ctx = lax.axis_index("ctx")
        self.dp, self.ctx = dp, ctx
        self.y, self.core = dp // 2, dp % 2
        self.z, self.x = ctx // 4, ctx % 4
        self.half = self.x // 2
        self.away = (self.core + self.half) % 2
        self.slot = self.z * 4 + self.x + self.away * (3 - 2 * self.x)
        self.mirror = self.z * 4 + 3 - self.x


def slot_of(z, x, core):
    away = (core + x // 2) % 2
    return z * 4 + x + away * (3 - 2 * x)


def greet(place):
    barrier = pltpu.get_barrier_semaphore()

    @pl.loop(0, 2 * SHARDS)
    def _(index):
        core, ctx = index // SHARDS, index % SHARDS
        own = jnp.logical_and(core == place.core, ctx == place.ctx)

        @pl.when(jnp.logical_not(own))
        def _():
            pl.semaphore_signal(
                barrier, inc=1, device_id=(place.y * 2 + core, ctx), device_id_type=MESH
            )

    for step in range(1, 4):
        other = ((place.y + step) % 4) * 2 + place.core
        pl.semaphore_signal(barrier, inc=1, device_id=(other, place.ctx), device_id_type=MESH)
    pl.semaphore_wait(barrier, 2 * SHARDS - 1 + 3)


def remote(src, dst, send_sem, recv_sem, dp, ctx):
    return pltpu.make_async_remote_copy(
        src_ref=src, dst_ref=dst, send_sem=send_sem, recv_sem=recv_sem, device_id=(dp, ctx), device_id_type=MESH
    )


def wait_bytes(ref, sem):
    pltpu.make_async_copy(ref, ref, sem).wait()


def rows_of(index, count):
    return pl.ds(pl.multiple_of(index * count, count), count)


def head_kernel(
    q_ref, k_ref, v_ref, stream_ref, gate_ref, mod_ref, hw_ref, pw_ref, uncond_ref, target_ref,
    qh_ref, kh_ref, vh_ref, w_ref, p_ref, gs_ref, loss_ref,
    moments, losses, mine, mine_loss, p_buf,
    a2a_send, a2a_recv, w_send, w_recv, m_send, m_recv, l_send, l_recv, p_send, p_recv,
):
    place = Place()
    tokens = stream_ref.shape[1]
    chunk = pw_ref.shape[1]
    cell_count = float(tokens * SHARDS * uncond_ref.shape[2])
    greet(place)

    def send_heads(src, dst, index):
        @pl.loop(0, SHARDS)
        def _(step):
            z = (place.z + step // 4) % 4
            x = 2 * place.core + (step // 2 + place.x) % 2
            core = (step + place.core) % 2
            slot = slot_of(z, x, core)
            own = jnp.logical_and(core == place.core, z * 4 + x == place.ctx)
            part = src.at[0, :, rows_of(slot, PAIR)]
            land = dst.at[rows_of(place.ctx, tokens), :]

            @pl.when(own)
            def _():
                pltpu.make_async_copy(part, land, a2a_recv.at[index]).start()

            @pl.when(jnp.logical_not(own))
            def _():
                remote(part, land, a2a_send.at[index], a2a_recv.at[index], place.y * 2 + core, z * 4 + x).start()

    own_cols = w_ref.at[:, rows_of(place.dp, chunk)]
    user = place.y * 2 + place.half

    @pl.when(place.away == 0)
    def _():
        pltpu.make_async_copy(pw_ref, own_cols, w_recv.at[0]).start()

    @pl.when(place.away == 1)
    def _():
        remote(pw_ref, own_cols, w_send.at[0], w_recv.at[0], user, place.ctx).start()

    remote(pw_ref, own_cols, w_send.at[1], w_recv.at[0], user, place.mirror).start()
    send_heads(q_ref, qh_ref, 0)
    send_heads(k_ref, kh_ref, 1)

    values = stream_ref[0].astype(jnp.float32)
    center = jnp.mean(values, axis=-1, keepdims=True)
    spread = jnp.mean(jnp.square(values - center), axis=-1, keepdims=True)
    inverse = lax.rsqrt(spread + norm_epsilon)
    normed = (values - center) * inverse
    scale_row = 1.0 + mod_ref[0, 1:2, :]
    hidden = (normed * scale_row + mod_ref[0, 0:1, :]).astype(jnp.bfloat16)
    cond_pred = dot_nt(hidden, hw_ref[...])
    uncond = uncond_ref[0]
    target = target_ref[0]
    guided = uncond + guidance * (cond_pred - uncond)

    def total(array):
        return jnp.sum(jnp.sum(array, axis=0, keepdims=True), axis=1, keepdims=True)

    lane = lax.broadcasted_iota(jnp.int32, (8, 128), 1)
    tile = jnp.zeros((8, 128), jnp.float32)
    for index, array in enumerate(
        (cond_pred, cond_pred * cond_pred, guided, guided * guided, guided * target)
    ):
        tile = jnp.where(lane == index, total(array), tile)
    mine[...] = tile

    def share(src, dst, send, recv):
        @pl.loop(1, SHARDS)
        def _(step):
            ctx = (place.ctx + step) % SHARDS
            remote(src, dst.at[place.ctx], send, recv, place.dp, ctx).start()

    def settle(dst, send, recv):
        wait_bytes(dst.at[pl.ds(0, SHARDS - 1)], recv)
        wait_bytes(dst.at[pl.ds(0, SHARDS - 1)], send)

    moments[place.ctx] = tile
    share(mine, moments, m_send, m_recv)
    send_heads(v_ref, vh_ref, 2)

    pair = w_ref.at[:, rows_of(place.y, 2 * chunk)]
    wait_bytes(pair, w_recv.at[0])
    for step in range(1, 4):
        other = ((place.y + step) % 4) * 2 + place.core
        remote(pair, pair, w_send.at[2], w_recv.at[1], other, place.ctx).start()

    settle(moments, m_send, m_recv)
    sums = jnp.sum(moments[...], axis=0)
    sum_cond, square_cond, sum_guided, square_guided, cross = [sums[0:1, i : i + 1] for i in range(5)]
    sigma_cond = sigma_of(sum_cond, square_cond, cell_count)
    sigma_guided = sigma_of(sum_guided, square_guided, cell_count)
    mix_ratio = rescale_mix * sigma_cond / sigma_guided + (1.0 - rescale_mix)
    final = mix_ratio * guided
    final_grad = 2.0 * (final - target)
    loss_tile = jnp.broadcast_to(total(jnp.square(final - target)), (8, 128))
    mine_loss[...] = loss_tile
    losses[place.ctx] = loss_tile
    share(mine_loss, losses, l_send, l_recv)
    slope_sum = 2.0 * (mix_ratio * square_guided - cross)
    guided_coef = slope_sum * rescale_mix * sigma_cond / (cell_count * sigma_guided * sigma_guided * sigma_guided)
    guided_grad = mix_ratio * final_grad - guided_coef * (guided - sum_guided / cell_count)
    cond_coef = slope_sum * rescale_mix / (cell_count * sigma_guided * sigma_cond)
    cond_grad = (guidance * guided_grad + cond_coef * (cond_pred - sum_cond / cell_count)).astype(jnp.bfloat16)
    head_grad = dot_nn(cond_grad, hw_ref[...]) * scale_row
    mean_one = jnp.mean(head_grad, axis=-1, keepdims=True)
    mean_two = jnp.mean(head_grad * normed, axis=-1, keepdims=True)
    stream_grad = (head_grad - mean_one - normed * mean_two) * inverse
    p_buf[...] = (gate_ref[...] * stream_grad).astype(jnp.bfloat16)

    @pl.when(place.away == 0)
    def _():
        pltpu.make_async_copy(p_buf, p_ref, p_recv).start()

    @pl.when(place.away == 1)
    def _():
        remote(p_buf, p_ref, p_send, p_recv, place.dp + 1 - 2 * place.core, place.mirror).start()

    gs_ref[0] = stream_grad.astype(jnp.bfloat16)
    settle(losses, l_send, l_recv)
    loss_ref[...] = jnp.sum(losses[...], axis=0) / cell_count

    wait_bytes(p_ref, p_recv)
    wait_bytes(w_ref.at[:, pl.ds(0, 6 * chunk)], w_recv.at[1])
    for index, ref in enumerate((qh_ref, kh_ref, vh_ref)):
        wait_bytes(ref, a2a_recv.at[index])

        @pl.loop(0, SHARDS - 1 + place.away)
        def _(step):
            wait_bytes(ref.at[pl.ds(0, tokens), :], a2a_send.at[index])

    wait_bytes(w_ref.at[:, pl.ds(0, chunk)], w_send.at[1])
    wait_bytes(w_ref.at[:, pl.ds(0, 6 * chunk)], w_send.at[2])

    @pl.when(place.away == 1)
    def _():
        wait_bytes(w_ref.at[:, pl.ds(0, chunk)], w_send.at[0])
        wait_bytes(p_ref, p_send)


def run_head(query, key, value, stream, gate, mod, head_weight, proj_weight, uncond, target):
    tokens, features = query.shape[1:]
    width = stream.shape[2]
    vmem = pl.BlockSpec(memory_space=pltpu.VMEM)
    hbm = pl.BlockSpec(memory_space=pl.ANY)
    slab = jax.ShapeDtypeStruct((tokens * SHARDS, PAIR), jnp.bfloat16)
    dma = pltpu.SemaphoreType.DMA
    return pl.pallas_call(
        head_kernel,
        out_shape=[
            slab, slab, slab,
            jax.ShapeDtypeStruct((PAIR, width), jnp.bfloat16),
            jax.ShapeDtypeStruct((tokens, width), jnp.bfloat16),
            jax.ShapeDtypeStruct(stream.shape, jnp.bfloat16),
            jax.ShapeDtypeStruct((8, 128), jnp.float32),
        ],
        in_specs=[hbm] * 3 + [vmem] * 7,
        out_specs=[hbm] * 5 + [vmem] * 2,
        scratch_shapes=[
            pltpu.VMEM((SHARDS, 8, 128), jnp.float32),
            pltpu.VMEM((SHARDS, 8, 128), jnp.float32),
            pltpu.VMEM((8, 128), jnp.float32),
            pltpu.VMEM((8, 128), jnp.float32),
            pltpu.VMEM((tokens, width), jnp.bfloat16),
            dma((3,)), dma((3,)), dma((3,)), dma((2,)),
            dma, dma, dma, dma, dma, dma,
        ],
        compiler_params=pltpu.CompilerParams(
            collective_id=0, has_side_effects=True, vmem_limit_bytes=60 * 2**20
        ),
    )(query, key, value, stream, gate, mod, head_weight, proj_weight, uncond, target)


def attention_kernel(
    q_ref, k_ref, v_ref, w_ref, own_ref,
    gq_ref, gk_ref, gv_ref, gp_ref,
    p_ref, v_ones, dk_sum, dv_sum, turned, dq_out, dk_out, dv_out, g_out, g_in, g_pair, g_last,
    ag_send, side_recv, next_recv, next2_recv, far_recv, sib_recv, own_sem,
    out_send, out_recv, g_send, g_recv, h_send, h_recv,
):
    place = Place()
    seq = q_ref.shape[0]
    tokens = seq // SHARDS
    width = p_ref.shape[1]
    half = tokens // 2
    tile = 2 * tokens
    greet(place)

    side_x = place.x + 1 - 2 * (place.x % 2)
    side = place.z * 4 + side_x
    sibling = place.dp + 1 - 2 * place.core

    def beside(step):
        return ((place.z + step) % 4) * 4 + place.x

    def block(z_step, x):
        return rows_of(slot_of((place.z + z_step) % 4, x, place.core), tokens)

    def spread(src, rows, recv, index):
        dst = p_ref.at[rows, :]
        remote(src, dst, ag_send.at[0], recv.at[3], place.dp, beside(1)).start()
        remote(src, dst, ag_send.at[0], recv.at[1], place.dp, beside(3)).start()

    def to_sibling(rows, index):
        remote(p_ref.at[rows, :], p_ref.at[rows, :], ag_send.at[1], sib_recv.at[index], sibling, place.ctx).start()

    def relay(x, far):
        low = p_ref.at[pl.ds(pl.multiple_of(slot_of((place.z + 3) % 4, x, place.core) * tokens, tokens), half), :]
        high = p_ref.at[
            pl.ds(pl.multiple_of(slot_of((place.z + 1) % 4, x, place.core) * tokens + half, half), half), :
        ]
        remote(low, low, ag_send.at[2], far_recv.at[far], place.dp, beside(1)).start()
        remote(high, high, ag_send.at[2], far_recv.at[far], place.dp, beside(3)).start()

    own_rows = block(0, place.x)
    side_rows = block(0, side_x)
    dst = p_ref.at[own_rows, :]
    remote(own_ref, dst, ag_send.at[1], side_recv, place.dp, side).start()
    spread(own_ref, own_rows, next_recv, 0)
    remote(own_ref, dst, ag_send.at[1], sib_recv.at[0], sibling, place.ctx).start()
    keep = pltpu.make_async_copy(own_ref, dst, own_sem)
    keep.start()

    for head in range(2):
        cols = slice(head * HD, (head + 1) * HD)
        v_ones[head, :, 0:HD] = v_ref[:, cols]
        v_ones[head, :, HD : 2 * HD] = jnp.ones((seq, HD), jnp.bfloat16)
    dk_sum[...] = jnp.zeros_like(dk_sum)
    dv_sum[...] = jnp.zeros_like(dv_sum)
    keep.wait()

    wait_bytes(dst, side_recv)
    spread(p_ref.at[side_rows, :], side_rows, next2_recv, 0)
    to_sibling(side_rows, 0)

    def send_rows(src, dst_ref, shard, index):
        own = jnp.logical_and(place.away == 0, shard == place.ctx)
        part = src.at[rows_of(shard, tokens), :]
        land = dst_ref.at[0, :, rows_of(place.slot, PAIR)]

        @pl.when(own)
        def _():
            pltpu.make_async_copy(part, land, out_recv.at[index]).start()

        @pl.when(jnp.logical_not(own))
        def _():
            remote(part, land, out_send.at[index], out_recv.at[index], place.y * 2 + place.half, shard).start()

    @pl.loop(0, 8)
    def _(step):
        turn = step // 2
        z_step = turn + (turn // 2) * (5 - 2 * turn)
        z = (place.z + z_step) % 4

        @pl.when(step == 1)
        def _():
            for near in (1, 3):
                wait_bytes(dst, next_recv.at[near])
            relay(place.x, 0)
            for near in (1, 3):
                to_sibling(block(near, place.x), near)

        @pl.when(step == 2)
        def _():
            for near in (1, 3):
                wait_bytes(dst, next2_recv.at[near])
            relay(side_x, 1)
            for near in (1, 3):
                to_sibling(block(near, side_x), near)

        @pl.when(step == 6)
        def _():
            for far, x in ((0, place.x), (1, side_x)):
                wait_bytes(dst, far_recv.at[far])
                to_sibling(block(2, x), 2)

        @pl.when(step % 2 == 1)
        def _():
            wait_bytes(p_ref.at[pl.ds(0, tile), :], sib_recv.at[z_step])

        rows = rows_of(z * 2 + (place.core + step) % 2, tile)
        out_grad = dot_nt(p_ref[rows, :], w_ref[...])
        outs = []
        for head in range(2):
            cols = slice(head * HD, (head + 1) * HD)
            q = q_ref[rows, cols]
            scores = dot_nt(q, k_ref[:, cols])
            top = jnp.max(scores, axis=-1, keepdims=True)
            weights = jnp.exp2((scores - top) * EXP2_SCALE).astype(jnp.bfloat16)
            sums = dot_nn(weights, v_ones[head])
            inverse = 1.0 / sums[:, HD:]
            out = sums[:, :HD] * inverse
            grad = (out_grad[:, cols] * inverse).astype(jnp.bfloat16)
            delta = jnp.sum(grad.astype(jnp.float32) * out, axis=-1, keepdims=True)
            prob_grad = dot_nt(grad, v_ref[:, cols]) - delta
            score_grad = (weights.astype(jnp.float32) * prob_grad).astype(jnp.bfloat16)
            dq_out[rows, cols] = (dot_nn(score_grad, k_ref[:, cols]) * SCALE).astype(jnp.bfloat16)
            dk_sum[head] += dot_nn(q.T, score_grad)
            dv_sum[head] += dot_nn(grad.T, weights)
            outs.append(out.astype(jnp.bfloat16))
        turned[:, rows] = jnp.concatenate(outs, axis=1).T

        @pl.loop(0, 2)
        def _(index):
            send_rows(dq_out, gq_ref, z * 4 + ((place.core + step) % 2) * 2 + index, 0)

    for head in range(2):
        cols = slice(head * HD, (head + 1) * HD)
        dk_out[:, cols] = (dk_sum[head] * SCALE).astype(jnp.bfloat16).T

    @pl.loop(0, SHARDS)
    def _(step):
        send_rows(dk_out, gk_ref, (place.ctx + step) % SHARDS, 1)

    for head in range(2):
        cols = slice(head * HD, (head + 1) * HD)
        dv_out[:, cols] = dv_sum[head].astype(jnp.bfloat16).T

    @pl.loop(0, SHARDS)
    def _(step):
        send_rows(dv_out, gv_ref, (place.ctx + step) % SHARDS, 2)

    wide = width // 4

    @pl.loop(1, 5)
    def _(step):
        y = (place.y + step) % 4
        g_out[y] = dot_nn(turned[...], p_ref[:, rows_of(y, wide)]).astype(jnp.bfloat16)

        @pl.when(step < 4)
        def _():
            remote(
                g_out.at[y], g_in.at[place.y], g_send, g_recv, y * 2 + place.core, place.ctx
            ).start()

    g_in[place.y] = g_out[place.y]
    wait_bytes(g_in.at[pl.ds(0, 3)], g_recv)
    total = jnp.sum(g_in[...].astype(jnp.float32), axis=0)
    g_pair[0] = total[:, : wide // 2].astype(jnp.bfloat16)
    g_pair[1] = total[:, wide // 2 :].astype(jnp.bfloat16)

    @pl.when(place.away == 0)
    def _():
        remote(g_pair.at[1 - place.core], g_last.at[0], h_send.at[0], h_recv.at[0], sibling, place.ctx).start()
        g_last[0] = g_pair[place.core]

    @pl.when(place.away == 1)
    def _():
        for core in range(2):
            remote(
                g_pair.at[core], g_last.at[1], h_send.at[core], h_recv.at[1], place.y * 2 + core, place.mirror
            ).start()
        wait_bytes(g_last.at[0], h_recv.at[0])

    wait_bytes(g_last.at[1], h_recv.at[1])
    gp_ref[...] = g_last[0].astype(jnp.float32) + g_last[1].astype(jnp.float32)

    wait_bytes(g_pair.at[0], h_send.at[0])

    @pl.when(place.away == 1)
    def _():
        wait_bytes(g_pair.at[1], h_send.at[1])

    wait_bytes(g_out.at[pl.ds(0, 3)], g_send)
    for index, ref in enumerate((gq_ref, gk_ref, gv_ref)):
        wait_bytes(ref, out_recv.at[index])

        @pl.loop(0, SHARDS - 1 + place.away)
        def _(step):
            wait_bytes(dq_out.at[pl.ds(0, tokens), :], out_send.at[index])

    wait_bytes(p_ref.at[pl.ds(0, 4 * tokens), :], ag_send.at[0])
    wait_bytes(p_ref.at[pl.ds(0, 9 * tokens), :], ag_send.at[1])
    wait_bytes(p_ref.at[pl.ds(0, 2 * tokens), :], ag_send.at[2])


def run_attention(query, key, value, proj_rows, own, tokens, features):
    seq = query.shape[0]
    width = own.shape[1]
    vmem = pl.BlockSpec(memory_space=pltpu.VMEM)
    hbm = pl.BlockSpec(memory_space=pl.ANY)
    grad = jax.ShapeDtypeStruct((1, tokens, features), jnp.bfloat16)
    dma = pltpu.SemaphoreType.DMA
    low = jnp.bfloat16
    return pl.pallas_call(
        attention_kernel,
        out_shape=[grad, grad, grad, jax.ShapeDtypeStruct((PAIR, width // 8), jnp.float32)],
        in_specs=[vmem] * 4 + [hbm],
        out_specs=[hbm] * 3 + [vmem],
        scratch_shapes=[
            pltpu.VMEM((seq, width), low),
            pltpu.VMEM((2, seq, PAIR), low),
            pltpu.VMEM((2, HD, seq), jnp.float32),
            pltpu.VMEM((2, HD, seq), jnp.float32),
            pltpu.VMEM((PAIR, seq), low),
            pltpu.VMEM((seq, PAIR), low),
            pltpu.VMEM((seq, PAIR), low),
            pltpu.VMEM((seq, PAIR), low),
            pltpu.VMEM((4, PAIR, width // 4), low),
            pltpu.VMEM((4, PAIR, width // 4), low),
            pltpu.VMEM((2, PAIR, width // 8), low),
            pltpu.VMEM((2, PAIR, width // 8), low),
            dma((3,)), dma, dma((4,)), dma((4,)), dma((2,)), dma((4,)), dma,
            dma((3,)), dma((3,)), dma, dma, dma((2,)), dma((2,)),
        ],
        compiler_params=pltpu.CompilerParams(
            collective_id=1, has_side_effects=True, vmem_limit_bytes=63 * 2**20
        ),
    )(query, key, value, proj_rows, own)


def per_device(
    query, key_states, value_states, block_out, gate_mod, head_mod, head_weight, proj_weight, uncond_pred, target
):
    query_heads, key_heads, value_heads, proj_rows, own, grad_stream, loss = run_head(
        query, key_states, value_states, block_out, gate_mod, head_mod, head_weight, proj_weight, uncond_pred, target
    )
    grads = run_attention(
        query_heads, key_heads, value_heads, proj_rows, own, query.shape[1], query.shape[2]
    )
    return (grads[0], grads[1], grads[2], grad_stream, grads[3], loss[0, 0:1])


def solution(mesh):
    return jax.shard_map(
        per_device,
        mesh=mesh,
        in_specs=(
            P("dp", "ctx", None),
            P("dp", "ctx", None),
            P("dp", "ctx", None),
            P("dp", "ctx", None),
            P("dp", None),
            P("dp", None, None),
            P(),
            P("ctx", "dp"),
            P("dp", "ctx", None),
            P("dp", "ctx", None),
        ),
        out_specs=(
            P("dp", "ctx", None),
            P("dp", "ctx", None),
            P("dp", "ctx", None),
            P("dp", "ctx", None),
            P("ctx", "dp"),
            P("dp"),
        ),
        check_vma=False,
    )
```

```python
import functools

import jax
import jax.numpy as jnp
from jax import lax
from jax.experimental import pallas as pl
from jax.experimental.pallas import tpu as pltpu
from jax.sharding import PartitionSpec as P

HD = 128
PAIR = 2 * HD
SHARDS = 16
SCALE = 1.0 / float(HD) ** 0.5
EXP2_SCALE = 1.4426950408889634 * SCALE
MESH = pl.DeviceIdType.MESH

guidance = 5.0
rescale_mix = 0.7
norm_epsilon = 1e-06
spread_epsilon = 1e-05


def dot_nt(left, right):
    return lax.dot_general(left, right, (((1,), (1,)), ((), ())), preferred_element_type=jnp.float32)


def dot_nn(left, right):
    return lax.dot_general(left, right, (((1,), (0,)), ((), ())), preferred_element_type=jnp.float32)


def sigma_of(first_sum, square_sum, cell_count):
    mean_value = first_sum / cell_count
    return jnp.sqrt(square_sum / cell_count - mean_value * mean_value + spread_epsilon)


class Place:
    def __init__(self):
        dp = lax.axis_index("dp")
        ctx = lax.axis_index("ctx")
        self.dp, self.ctx = dp, ctx
        self.y, self.core = dp // 2, dp % 2
        self.z, self.x = ctx // 4, ctx % 4
        self.half = self.x // 2
        self.away = (self.core + self.half) % 2
        self.slot = self.z * 4 + self.x + self.away * (3 - 2 * self.x)
        self.mirror = self.z * 4 + 3 - self.x


def slot_of(z, x, core):
    away = (core + x // 2) % 2
    return z * 4 + x + away * (3 - 2 * x)


def greet(place):
    barrier = pltpu.get_barrier_semaphore()

    @pl.loop(0, 2 * SHARDS)
    def _(index):
        core, ctx = index // SHARDS, index % SHARDS
        own = jnp.logical_and(core == place.core, ctx == place.ctx)

        @pl.when(jnp.logical_not(own))
        def _():
            pl.semaphore_signal(
                barrier, inc=1, device_id=(place.y * 2 + core, ctx), device_id_type=MESH
            )

    for step in range(1, 4):
        other = ((place.y + step) % 4) * 2 + place.core
        pl.semaphore_signal(barrier, inc=1, device_id=(other, place.ctx), device_id_type=MESH)
    pl.semaphore_wait(barrier, 2 * SHARDS - 1 + 3)


def remote(src, dst, send_sem, recv_sem, dp, ctx):
    return pltpu.make_async_remote_copy(
        src_ref=src, dst_ref=dst, send_sem=send_sem, recv_sem=recv_sem, device_id=(dp, ctx), device_id_type=MESH
    )


def wait_bytes(ref, sem):
    pltpu.make_async_copy(ref, ref, sem).wait()


def rows_of(index, count):
    return pl.ds(pl.multiple_of(index * count, count), count)


def kernel(
    q_arg, k_arg, v_arg, stream_ref, gate_ref, mod_ref, hw_ref, pw_ref, uncond_ref, target_ref,
    gq_ref, gk_ref, gv_ref, gs_ref, gp_ref, loss_ref,
    q_ref, k_ref, v_ref, w_ref, p_ref, p_buf, moments, losses, mine, mine_loss,
    v_ones, kept, kept_out, kept_inverse, dk_sum, dv_sum, turned, g_out, g_in, g_pair, g_last,
    a2a_send, a2a_recv, w_send, w_recv, m_send, m_recv, l_send, l_recv, p_send, p_recv,
    ag_send, own_send, side_recv, own_x_recv, side_x_recv, far_x_recv, near_z_recv, far_z_recv, side_z_recv, sib_recv,
    out_send, out_recv, g_send, g_recv, h_send, h_recv,
):
    place = Place()
    tokens = stream_ref.shape[1]
    seq, width = p_ref.shape
    chunk = pw_ref.shape[1]
    cell_count = float(seq * uncond_ref.shape[1])
    half = tokens // 2
    tile = 2 * tokens
    first_cols = (width // 128 * 11 // 20) * 128
    x_cols, z_cols = pl.ds(0, first_cols), pl.ds(first_cols, width - first_cols)
    greet(place)

    def send_heads(src, dst, index):
        @pl.loop(0, SHARDS)
        def _(step):
            z = (place.z + step // 4) % 4
            x = 2 * place.core + (step // 2 + place.x) % 2
            core = (step + place.core) % 2
            slot = slot_of(z, x, core)
            own = jnp.logical_and(core == place.core, z * 4 + x == place.ctx)
            part = src.at[0, :, rows_of(slot, PAIR)]
            land = dst.at[rows_of(place.ctx, tokens), :]

            @pl.when(own)
            def _():
                pltpu.make_async_copy(part, land, a2a_recv.at[index]).start()

            @pl.when(jnp.logical_not(own))
            def _():
                remote(part, land, a2a_send.at[index], a2a_recv.at[index], place.y * 2 + core, z * 4 + x).start()

    own_cols = w_ref.at[:, rows_of(place.dp, chunk)]
    user = place.y * 2 + place.half

    @pl.when(place.away == 0)
    def _():
        pltpu.make_async_copy(pw_ref, own_cols, w_recv.at[0]).start()

    @pl.when(place.away == 1)
    def _():
        remote(pw_ref, own_cols, w_send.at[0], w_recv.at[0], user, place.ctx).start()

    remote(pw_ref, own_cols, w_send.at[1], w_recv.at[0], user, place.mirror).start()
    send_heads(q_arg, q_ref, 0)

    step_cols = PAIR
    pieces = [slice(start, start + step_cols) for start in range(0, width, step_cols)]

    def values(cols):
        return stream_ref[0, :, cols].astype(jnp.float32)

    def row_mean(term):
        folded = jnp.zeros((tokens, HD), jnp.float32)
        for cols in pieces:
            piece = term(cols)
            folded += piece[:, :HD] + piece[:, HD:]
        return jnp.sum(folded, axis=-1, keepdims=True) / width

    center = row_mean(values)
    inverse = lax.rsqrt(row_mean(lambda cols: jnp.square(values(cols) - center)) + norm_epsilon)

    def normed(cols):
        return (values(cols) - center) * inverse

    for cols in pieces:
        hidden = normed(cols) * (1.0 + mod_ref[0, 1:2, cols]) + mod_ref[0, 0:1, cols]
        p_buf[:, cols] = hidden.astype(jnp.bfloat16)
    cond_pred = dot_nt(p_buf[...], hw_ref[...]).T
    uncond = uncond_ref[0]
    target = target_ref[0]
    guided = uncond + guidance * (cond_pred - uncond)

    def total(array):
        return jnp.sum(jnp.sum(array, axis=0, keepdims=True), axis=1, keepdims=True)

    lane = lax.broadcasted_iota(jnp.int32, (8, 128), 1)
    tally = jnp.zeros((8, 128), jnp.float32)
    for index, array in enumerate(
        (cond_pred, cond_pred * cond_pred, guided, guided * guided, guided * target)
    ):
        tally = jnp.where(lane == index, total(array), tally)
    mine[...] = tally

    def share(src, dst, send, recv):
        @pl.loop(1, SHARDS)
        def _(step):
            ctx = (place.ctx + step) % SHARDS
            remote(src, dst.at[place.ctx], send, recv, place.dp, ctx).start()

    def settle(dst, send, recv):
        wait_bytes(dst.at[pl.ds(0, SHARDS - 1)], recv)
        wait_bytes(dst.at[pl.ds(0, SHARDS - 1)], send)

    moments[place.ctx] = tally
    share(mine, moments, m_send, m_recv)

    @pl.when(place.away == 0)
    def _():
        send_heads(k_arg, k_ref, 1)


    settle(moments, m_send, m_recv)
    sums = jnp.sum(moments[...], axis=0)
    sum_cond, square_cond, sum_guided, square_guided, cross = [sums[0:1, i : i + 1] for i in range(5)]
    sigma_cond = sigma_of(sum_cond, square_cond, cell_count)
    sigma_guided = sigma_of(sum_guided, square_guided, cell_count)
    mix_ratio = rescale_mix * sigma_cond / sigma_guided + (1.0 - rescale_mix)
    final = mix_ratio * guided
    final_grad = 2.0 * (final - target)
    loss_tile = jnp.broadcast_to(total(jnp.square(final - target)), (8, 128))
    mine_loss[...] = loss_tile
    losses[place.ctx] = loss_tile
    slope_sum = 2.0 * (mix_ratio * square_guided - cross)
    guided_coef = slope_sum * rescale_mix * sigma_cond / (cell_count * sigma_guided * sigma_guided * sigma_guided)
    guided_grad = mix_ratio * final_grad - guided_coef * (guided - sum_guided / cell_count)
    cond_coef = slope_sum * rescale_mix / (cell_count * sigma_guided * sigma_cond)
    cond_grad = (guidance * guided_grad + cond_coef * (cond_pred - sum_cond / cell_count)).astype(jnp.bfloat16)
    cond_rows = cond_grad.T

    def head_grad(cols):
        return dot_nn(cond_rows, hw_ref[:, cols]) * (1.0 + mod_ref[0, 1:2, cols])

    mean_one = row_mean(head_grad)
    mean_two = row_mean(lambda cols: head_grad(cols) * normed(cols))
    for cols in pieces:
        stream_grad = (head_grad(cols) - mean_one - normed(cols) * mean_two) * inverse
        p_buf[:, cols] = (gate_ref[:, cols] * stream_grad).astype(jnp.bfloat16)
        gs_ref[0, :, cols] = stream_grad.astype(jnp.bfloat16)

    side_x = place.x + 1 - 2 * (place.x % 2)
    side = place.z * 4 + side_x
    sibling = place.dp + 1 - 2 * place.core
    x_send, z_send = ag_send.at[0], ag_send.at[1]

    def beside(step):
        return ((place.z + step) % 4) * 4 + place.x

    def start(z_step, x):
        return slot_of((place.z + z_step) % 4, x, place.core) * tokens

    def part(z_step, x, cols, offset=0, count=None):
        return p_ref.at[pl.ds(pl.multiple_of(start(z_step, x) + offset, half), count or tokens), cols]

    def hand(ref, send, recv, dp, ctx):
        remote(ref, ref, send, recv, dp, ctx).start()

    def to_neighbours(ref, send, recv):
        hand(ref, send, recv.at[3], place.dp, beside(1))
        hand(ref, send, recv.at[1], place.dp, beside(3))

    def relay(x, cols, send, recv):
        hand(part(3, x, cols, 0, half), send, recv, place.dp, beside(1))
        hand(part(1, x, cols, half, half), send, recv, place.dp, beside(3))

    def to_sibling(ref, send, z_step):
        hand(ref, send, sib_recv.at[z_step], sibling, place.ctx)

    own = p_ref.at[pl.ds(pl.multiple_of(start(0, place.x), tokens), tokens), :]

    @pl.when(place.away == 0)
    def _():
        pltpu.make_async_copy(p_buf, own, p_recv).start()

    @pl.when(place.away == 1)
    def _():
        land = p_ref.at[rows_of(place.ctx, tokens), :]
        remote(p_buf, land, p_send, p_recv, sibling, place.mirror).start()

    @pl.when(place.away == 0)
    def _():
        send_heads(v_arg, v_ref, 2)


    pair = w_ref.at[:, rows_of(place.y, 2 * chunk)]
    wait_bytes(pair, w_recv.at[0])
    for step in range(1, 4):
        other = ((place.y + step) % 4) * 2 + place.core
        remote(pair, pair, w_send.at[2], w_recv.at[1], other, place.ctx).start()

    wait_bytes(own, p_recv)
    hand(part(0, place.x, x_cols), x_send, side_recv, place.dp, side)
    to_neighbours(part(0, place.x, z_cols), z_send, near_z_recv)
    to_neighbours(part(0, place.x, x_cols), x_send, own_x_recv)
    hand(part(0, place.x, z_cols), z_send, side_z_recv.at[0], place.dp, side)
    hand(own, own_send, sib_recv.at[0], sibling, place.ctx)
    share(mine_loss, losses, l_send, l_recv)

    @pl.when(place.away == 1)
    def _():
        wait_bytes(p_buf, p_send)
        send_heads(k_arg, k_ref, 1)
        send_heads(v_arg, v_ref, 2)


    def rows_at(z_step, which):
        return rows_of(((place.z + z_step) % 4) * 2 + which, tile)

    def forward(rows, keep):
        outs = []
        for head in range(2):
            cols = slice(head * HD, (head + 1) * HD)
            scores = dot_nt(q_ref[rows, cols], k_ref[:, cols])
            top = jnp.max(scores, axis=-1, keepdims=True)
            weights = jnp.exp2((scores - top) * EXP2_SCALE).astype(jnp.bfloat16)
            kept[keep, head] = weights
            sums = dot_nn(weights, v_ones[head])
            inverse = 1.0 / sums[:, HD:]
            out = sums[:, :HD] * inverse
            kept_out[keep, head] = out
            kept_inverse[keep, head] = inverse
            outs.append(out.astype(jnp.bfloat16))
        turned[:, rows] = jnp.concatenate(outs, axis=1).T

    def backward(rows, keep):
        out_grad = dot_nt(p_ref[rows, :], w_ref[...])
        for head in range(2):
            cols = slice(head * HD, (head + 1) * HD)
            q = q_ref[rows, cols]
            grad = (out_grad[:, cols] * kept_inverse[keep, head]).astype(jnp.bfloat16)
            delta = jnp.sum(grad.astype(jnp.float32) * kept_out[keep, head], axis=-1, keepdims=True)
            prob_grad = dot_nt(grad, v_ref[:, cols]) - delta
            weights = kept[keep, head]
            score_grad = (weights.astype(jnp.float32) * prob_grad).astype(jnp.bfloat16)
            dk_sum[head] += dot_nn(q.T, score_grad)
            dv_sum[head] += dot_nn(grad.T, weights)
            q_ref[rows, cols] = (dot_nn(score_grad, k_ref[:, cols]) * SCALE).astype(jnp.bfloat16)

    for near in (1, 3):
        wait_bytes(part(near, place.x, z_cols), near_z_recv.at[near])
    hand(part(1, place.x, z_cols), z_send, side_z_recv.at[1], place.dp, side)
    for near in (1, 3):
        to_sibling(part(near, place.x, z_cols), z_send, near)
    wait_bytes(part(0, side_x, x_cols), side_recv)
    to_neighbours(part(0, side_x, x_cols), x_send, side_x_recv)
    to_sibling(part(0, side_x, x_cols), x_send, 0)

    wait_bytes(part(0, side_x, z_cols), side_z_recv.at[0])
    hand(part(3, place.x, z_cols), z_send, side_z_recv.at[3], place.dp, side)
    relay(place.x, z_cols, z_send, far_z_recv)
    to_sibling(part(0, side_x, z_cols), z_send, 0)
    for near in (1, 3):
        wait_bytes(part(near, place.x, x_cols), own_x_recv.at[near])
    for near in (1, 3):
        to_sibling(part(near, place.x, x_cols), x_send, near)

    dk_sum[...] = jnp.zeros_like(dk_sum)
    dv_sum[...] = jnp.zeros_like(dv_sum)
    for index, ref in enumerate((q_ref, k_ref, v_ref)):
        wait_bytes(ref, a2a_recv.at[index])
    for head in range(2):
        v_ones[head, :, 0:HD] = v_ref[:, head * HD : (head + 1) * HD]
        v_ones[head, :, HD : 2 * HD] = jnp.ones((seq, HD), jnp.bfloat16)

    @pl.loop(0, 2)
    def _(which):
        forward(rows_at(2, which), which)

    wait_bytes(w_ref.at[:, pl.ds(0, 6 * chunk)], w_recv.at[1])

    @pl.loop(0, 6)
    def _(step):
        turn = step // 2
        z_step = turn + turn // 2

        @pl.when(step == 2)
        def _():
            wait_bytes(part(2, place.x, z_cols), far_z_recv)
            relay(place.x, x_cols, x_send, far_x_recv.at[0])
            hand(part(2, place.x, z_cols), z_send, side_z_recv.at[2], place.dp, side)
            to_sibling(part(2, place.x, z_cols), z_send, 2)
            wait_bytes(part(1, side_x, z_cols), side_z_recv.at[1])
            to_sibling(part(1, side_x, z_cols), z_send, 1)
            for near in (1, 3):
                wait_bytes(part(near, side_x, x_cols), side_x_recv.at[near])
            relay(side_x, x_cols, x_send, far_x_recv.at[1])
            for near in (1, 3):
                to_sibling(part(near, side_x, x_cols), x_send, near)

        @pl.when(step == 4)
        def _():
            wait_bytes(part(3, side_x, z_cols), side_z_recv.at[3])
            to_sibling(part(3, side_x, z_cols), z_send, 3)

        @pl.when(step % 2 == 1)
        def _():
            wait_bytes(p_ref.at[pl.ds(0, tile), :], sib_recv.at[z_step])

        rows = rows_at(z_step, (place.core + step) % 2)
        forward(rows, 2)
        backward(rows, 2)

    for far, x in ((0, place.x), (1, side_x)):
        wait_bytes(part(2, x, x_cols), far_x_recv.at[far])
        to_sibling(part(2, x, x_cols), x_send, 2)
    wait_bytes(part(2, side_x, z_cols), side_z_recv.at[2])
    to_sibling(part(2, side_x, z_cols), z_send, 2)

    def send_rows(src, dst_ref, shard, index):
        own_shard = jnp.logical_and(place.away == 0, shard == place.ctx)
        rows = src.at[rows_of(shard, tokens), :]
        land = dst_ref.at[0, :, rows_of(place.slot, PAIR)]

        @pl.when(own_shard)
        def _():
            pltpu.make_async_copy(rows, land, out_recv.at[index]).start()

        @pl.when(jnp.logical_not(own_shard))
        def _():
            remote(rows, land, out_send.at[index], out_recv.at[index], user, shard).start()

    @pl.loop(0, 12)
    def _(step):
        turn = step // 4
        send_rows(q_ref, gq_ref, ((place.z + turn + turn // 2) % 4) * 4 + (step + place.x) % 4, 0)

    wait_bytes(p_ref.at[pl.ds(0, tile), :], sib_recv.at[2])

    wide = width // 4

    @pl.loop(1, 5)
    def _(step):
        y = (place.y + step) % 4
        g_out[y] = dot_nn(turned[...], p_ref[:, rows_of(y, wide)]).astype(jnp.bfloat16)

        @pl.when(step < 4)
        def _():
            remote(g_out.at[y], g_in.at[place.y], g_send, g_recv, y * 2 + place.core, place.ctx).start()

    g_in[place.y] = g_out[place.y]

    @pl.loop(0, 2)
    def _(which):
        backward(rows_at(2, which), which)

    @pl.loop(0, 4)
    def _(step):
        send_rows(q_ref, gq_ref, ((place.z + 2) % 4) * 4 + (step + place.x) % 4, 0)

    for head in range(2):
        cols = slice(head * HD, (head + 1) * HD)
        k_ref[:, cols] = (dk_sum[head] * SCALE).astype(jnp.bfloat16).T

    @pl.loop(0, SHARDS)
    def _(step):
        send_rows(k_ref, gk_ref, (place.ctx + step) % SHARDS, 1)

    for head in range(2):
        cols = slice(head * HD, (head + 1) * HD)
        v_ref[:, cols] = dv_sum[head].astype(jnp.bfloat16).T

    @pl.loop(0, SHARDS)
    def _(step):
        send_rows(v_ref, gv_ref, (place.ctx + step) % SHARDS, 2)

    settle(losses, l_send, l_recv)
    loss_ref[...] = jnp.sum(losses[...], axis=0) / cell_count

    wait_bytes(g_in.at[pl.ds(0, 3)], g_recv)
    total_g = jnp.sum(g_in[...].astype(jnp.float32), axis=0)
    g_pair[0] = total_g[:, : wide // 2].astype(jnp.bfloat16)
    g_pair[1] = total_g[:, wide // 2 :].astype(jnp.bfloat16)

    @pl.when(place.away == 0)
    def _():
        remote(g_pair.at[1 - place.core], g_last.at[0], h_send.at[0], h_recv.at[0], sibling, place.ctx).start()
        g_last[0] = g_pair[place.core]

    @pl.when(place.away == 1)
    def _():
        for core in range(2):
            remote(
                g_pair.at[core], g_last.at[1], h_send.at[core], h_recv.at[1], place.y * 2 + core, place.mirror
            ).start()
        wait_bytes(g_last.at[0], h_recv.at[0])

    wait_bytes(g_last.at[1], h_recv.at[1])
    gp_ref[...] = g_last[0].astype(jnp.float32) + g_last[1].astype(jnp.float32)

    for index, ref in enumerate((gq_ref, gk_ref, gv_ref)):
        wait_bytes(ref, out_recv.at[index])

    @pl.loop(0, SHARDS - 1 + place.away)
    def _(step):
        for index in range(3):
            wait_bytes(q_ref.at[pl.ds(0, tokens), :], a2a_send.at[index])
            wait_bytes(q_ref.at[pl.ds(0, tokens), :], out_send.at[index])

    wait_bytes(g_pair.at[0], h_send.at[0])
    wait_bytes(g_out.at[pl.ds(0, 3)], g_send)
    wait_bytes(w_ref.at[:, pl.ds(0, chunk)], w_send.at[1])
    wait_bytes(w_ref.at[:, pl.ds(0, 6 * chunk)], w_send.at[2])

    @pl.when(place.away == 1)
    def _():
        wait_bytes(g_pair.at[1], h_send.at[1])
        wait_bytes(w_ref.at[:, pl.ds(0, chunk)], w_send.at[0])

    wait_bytes(p_buf, own_send)
    wait_bytes(p_ref.at[pl.ds(0, 14 * tokens), x_cols], x_send)
    wait_bytes(p_ref.at[pl.ds(0, 14 * tokens), z_cols], z_send)


def hand_over(*refs):
    sources, loss, results, loss_out = refs[:5], refs[5], refs[6:11], refs[11]
    held, arrived, left = refs[12:17], refs[17], refs[18]
    fetches = [pltpu.make_async_copy(sources[i], held[i], arrived.at[i]) for i in range(5)]
    stores = [pltpu.make_async_copy(held[i], results[i], left.at[i]) for i in range(5)]
    for fetch in fetches:
        fetch.start()
    loss_out[0] = loss[0, 0]
    for fetch, store in zip(fetches, stores):
        fetch.wait()
        store.start()
    for store in stores:
        store.wait()


def per_device(
    query, key_states, value_states, block_out, gate_mod, head_mod, head_weight, proj_weight, uncond_pred, target
):
    tokens, features = query.shape[1:]
    seq = tokens * SHARDS
    width = block_out.shape[2]
    vmem = pl.BlockSpec(memory_space=pltpu.VMEM)
    hbm = pl.BlockSpec(memory_space=pl.ANY)
    grad = jax.ShapeDtypeStruct(query.shape, jnp.bfloat16)
    dma = pltpu.SemaphoreType.DMA
    low, wide = jnp.bfloat16, jnp.float32
    grads = pl.pallas_call(
        kernel,
        out_shape=[
            grad, grad, grad,
            jax.ShapeDtypeStruct(block_out.shape, low),
            jax.ShapeDtypeStruct(proj_weight.shape, wide),
            jax.ShapeDtypeStruct((8, 128), wide),
        ],
        in_specs=[hbm] * 3 + [vmem] * 7,
        out_specs=[hbm] * 3 + [vmem] * 3,
        scratch_shapes=[
            pltpu.VMEM((seq, PAIR), low),
            pltpu.VMEM((seq, PAIR), low),
            pltpu.VMEM((seq, PAIR), low),
            pltpu.VMEM((PAIR, width), low),
            pltpu.VMEM((seq, width), low),
            pltpu.VMEM((tokens, width), low),
            pltpu.VMEM((SHARDS, 8, 128), wide),
            pltpu.VMEM((SHARDS, 8, 128), wide),
            pltpu.VMEM((8, 128), wide),
            pltpu.VMEM((8, 128), wide),
            pltpu.VMEM((2, seq, PAIR), low),
            pltpu.VMEM((3, 2, 2 * tokens, seq), low),
            pltpu.VMEM((3, 2, 2 * tokens, HD), wide),
            pltpu.VMEM((3, 2, 2 * tokens, HD), wide),
            pltpu.VMEM((2, HD, seq), wide),
            pltpu.VMEM((2, HD, seq), wide),
            pltpu.VMEM((PAIR, seq), low),
            pltpu.VMEM((4, PAIR, width // 4), low),
            pltpu.VMEM((4, PAIR, width // 4), low),
            pltpu.VMEM((2, PAIR, width // 8), low),
            pltpu.VMEM((2, PAIR, width // 8), low),
            dma((3,)), dma((3,)), dma((3,)), dma((2,)),
            dma, dma, dma, dma, dma, dma,
            dma((2,)), dma, dma, dma((4,)), dma((4,)), dma((2,)), dma((4,)), dma, dma((4,)), dma((4,)),
            dma((3,)), dma((3,)), dma, dma, dma((2,)), dma((2,)),
        ],
        compiler_params=pltpu.CompilerParams(
            collective_id=0, has_side_effects=True, vmem_limit_bytes=63 * 2**20
        ),
    )(
        query, key_states, value_states, block_out, gate_mod, head_mod, head_weight, proj_weight,
        jnp.swapaxes(uncond_pred, 1, 2), jnp.swapaxes(target, 1, 2),
    )
    smem = pl.BlockSpec(memory_space=pltpu.SMEM)
    return pl.pallas_call(
        hand_over,
        out_shape=[jax.ShapeDtypeStruct(array.shape, array.dtype) for array in grads[:5]]
        + [jax.ShapeDtypeStruct((1,), wide)],
        in_specs=[hbm] * 5 + [smem],
        out_specs=[hbm] * 5 + [smem],
        scratch_shapes=[pltpu.VMEM(array.shape, array.dtype) for array in grads[:5]] + [dma((5,)), dma((5,))],
        compiler_params=pltpu.CompilerParams(vmem_limit_bytes=63 * 2**20),
    )(*grads)


def solution(mesh):
    return jax.shard_map(
        per_device,
        mesh=mesh,
        in_specs=(
            P("dp", "ctx", None),
            P("dp", "ctx", None),
            P("dp", "ctx", None),
            P("dp", "ctx", None),
            P("dp", None),
            P("dp", None, None),
            P(),
            P("ctx", "dp"),
            P("dp", "ctx", None),
            P("dp", "ctx", None),
        ),
        out_specs=(
            P("dp", "ctx", None),
            P("dp", "ctx", None),
            P("dp", "ctx", None),
            P("dp", "ctx", None),
            P("ctx", "dp"),
            P("dp"),
        ),
        check_vma=False,
    )
```

```python
import functools

import jax
import jax.numpy as jnp
from jax import lax
from jax.experimental import pallas as pl
from jax.experimental.pallas import tpu as pltpu
from jax.sharding import PartitionSpec as P

HD = 128
PAIR = 2 * HD
SHARDS = 16
SCALE = 1.0 / float(HD) ** 0.5
EXP2_SCALE = 1.4426950408889634 * SCALE
MESH = pl.DeviceIdType.MESH

guidance = 5.0
rescale_mix = 0.7
norm_epsilon = 1e-06
spread_epsilon = 1e-05


def dot_nt(left, right):
    return lax.dot_general(left, right, (((1,), (1,)), ((), ())), preferred_element_type=jnp.float32)


def dot_nn(left, right):
    return lax.dot_general(left, right, (((1,), (0,)), ((), ())), preferred_element_type=jnp.float32)


def sigma_of(first_sum, square_sum, cell_count):
    mean_value = first_sum / cell_count
    return jnp.sqrt(square_sum / cell_count - mean_value * mean_value + spread_epsilon)


class Place:
    def __init__(self):
        dp = lax.axis_index("dp")
        ctx = lax.axis_index("ctx")
        self.dp, self.ctx = dp, ctx
        self.y, self.core = dp // 2, dp % 2
        self.z, self.x = ctx // 4, ctx % 4
        self.half = self.x // 2
        self.away = (self.core + self.half) % 2
        self.slot = self.z * 4 + self.x + self.away * (3 - 2 * self.x)
        self.mirror = self.z * 4 + 3 - self.x


def slot_of(z, x, core):
    away = (core + x // 2) % 2
    return z * 4 + x + away * (3 - 2 * x)


def greet(place):
    barrier = pltpu.get_barrier_semaphore()

    @pl.loop(0, 2 * SHARDS)
    def _(index):
        core, ctx = index // SHARDS, index % SHARDS
        own = jnp.logical_and(core == place.core, ctx == place.ctx)

        @pl.when(jnp.logical_not(own))
        def _():
            pl.semaphore_signal(
                barrier, inc=1, device_id=(place.y * 2 + core, ctx), device_id_type=MESH
            )

    for step in range(1, 4):
        other = ((place.y + step) % 4) * 2 + place.core
        pl.semaphore_signal(barrier, inc=1, device_id=(other, place.ctx), device_id_type=MESH)
    pl.semaphore_wait(barrier, 2 * SHARDS - 1 + 3)


def remote(src, dst, send_sem, recv_sem, dp, ctx):
    return pltpu.make_async_remote_copy(
        src_ref=src, dst_ref=dst, send_sem=send_sem, recv_sem=recv_sem, device_id=(dp, ctx), device_id_type=MESH
    )


def wait_bytes(ref, sem):
    pltpu.make_async_copy(ref, ref, sem).wait()


def rows_of(index, count):
    return pl.ds(pl.multiple_of(index * count, count), count)


def kernel(
    q_arg, k_arg, v_arg, stream_ref, gate_ref, mod_ref, hw_ref, pw_ref, uncond_ref, target_ref,
    gq_ref, gk_ref, gv_ref, gs_ref, gp_ref, loss_ref,
    q_ref, k_ref, v_ref, w_ref, p_ref, p_buf, moments, losses, mine, mine_loss,
    v_ones, last_grad, kept, kept_out, kept_inverse, dk_sum, dv_sum, turned, g_out, g_in, g_pair, g_last,
    a2a_send, a2a_recv, w_send, w_recv, m_send, m_recv, l_send, l_recv, p_send, p_recv,
    ag_send, own_send, side_recv, own_x_recv, side_x_recv, far_x_recv, near_z_recv, far_z_recv, side_z_recv, sib_recv,
    out_send, out_recv, g_send, g_recv, h_send, h_recv,
):
    place = Place()
    tokens = stream_ref.shape[1]
    seq, width = p_ref.shape
    chunk = pw_ref.shape[1]
    cell_count = float(seq * uncond_ref.shape[1])
    half = tokens // 2
    tile = 2 * tokens
    first_cols = (width // 128 * 28 // 40) * 128
    x_cols, z_cols = pl.ds(0, first_cols), pl.ds(first_cols, width - first_cols)
    greet(place)

    def send_heads(src, dst, index):
        @pl.loop(0, SHARDS)
        def _(step):
            z = (place.z + step // 4) % 4
            x = 2 * place.core + (step // 2 + place.x) % 2
            core = (step + place.core) % 2
            slot = slot_of(z, x, core)
            own = jnp.logical_and(core == place.core, z * 4 + x == place.ctx)
            part = src.at[0, :, rows_of(slot, PAIR)]
            land = dst.at[rows_of(place.ctx, tokens), :]

            @pl.when(own)
            def _():
                pltpu.make_async_copy(part, land, a2a_recv.at[index]).start()

            @pl.when(jnp.logical_not(own))
            def _():
                remote(part, land, a2a_send.at[index], a2a_recv.at[index], place.y * 2 + core, z * 4 + x).start()

    own_cols = w_ref.at[:, rows_of(place.dp, chunk)]
    user = place.y * 2 + place.half

    @pl.when(place.away == 0)
    def _():
        pltpu.make_async_copy(pw_ref, own_cols, w_recv.at[0]).start()

    @pl.when(place.away == 1)
    def _():
        remote(pw_ref, own_cols, w_send.at[0], w_recv.at[0], user, place.ctx).start()

    remote(pw_ref, own_cols, w_send.at[1], w_recv.at[0], user, place.mirror).start()
    send_heads(q_arg, q_ref, 0)

    step_cols = PAIR
    pieces = [slice(start, start + step_cols) for start in range(0, width, step_cols)]

    def values(cols):
        return stream_ref[0, :, cols].astype(jnp.float32)

    def row_mean(term):
        folded = jnp.zeros((tokens, HD), jnp.float32)
        for cols in pieces:
            piece = term(cols)
            folded += piece[:, :HD] + piece[:, HD:]
        return jnp.sum(folded, axis=-1, keepdims=True) / width

    center = row_mean(values)
    inverse = lax.rsqrt(row_mean(lambda cols: jnp.square(values(cols) - center)) + norm_epsilon)

    def normed(cols):
        return (values(cols) - center) * inverse

    for cols in pieces:
        hidden = normed(cols) * (1.0 + mod_ref[0, 1:2, cols]) + mod_ref[0, 0:1, cols]
        p_buf[:, cols] = hidden.astype(jnp.bfloat16)
    cond_pred = dot_nt(p_buf[...], hw_ref[...]).T
    uncond = uncond_ref[0]
    target = target_ref[0]
    guided = uncond + guidance * (cond_pred - uncond)

    def total(array):
        return jnp.sum(jnp.sum(array, axis=0, keepdims=True), axis=1, keepdims=True)

    lane = lax.broadcasted_iota(jnp.int32, (8, 128), 1)
    tally = jnp.zeros((8, 128), jnp.float32)
    for index, array in enumerate(
        (cond_pred, cond_pred * cond_pred, guided, guided * guided, guided * target)
    ):
        tally = jnp.where(lane == index, total(array), tally)
    mine[...] = tally

    def share(src, dst, send, recv):
        @pl.loop(1, SHARDS)
        def _(step):
            ctx = (place.ctx + step) % SHARDS
            remote(src, dst.at[place.ctx], send, recv, place.dp, ctx).start()

    def settle(dst, send, recv):
        wait_bytes(dst.at[pl.ds(0, SHARDS - 1)], recv)
        wait_bytes(dst.at[pl.ds(0, SHARDS - 1)], send)

    moments[place.ctx] = tally
    share(mine, moments, m_send, m_recv)

    @pl.when(place.away == 0)
    def _():
        send_heads(k_arg, k_ref, 1)


    settle(moments, m_send, m_recv)
    sums = jnp.sum(moments[...], axis=0)
    sum_cond, square_cond, sum_guided, square_guided, cross = [sums[0:1, i : i + 1] for i in range(5)]
    sigma_cond = sigma_of(sum_cond, square_cond, cell_count)
    sigma_guided = sigma_of(sum_guided, square_guided, cell_count)
    mix_ratio = rescale_mix * sigma_cond / sigma_guided + (1.0 - rescale_mix)
    final = mix_ratio * guided
    final_grad = 2.0 * (final - target)
    loss_tile = jnp.broadcast_to(total(jnp.square(final - target)), (8, 128))
    mine_loss[...] = loss_tile
    losses[place.ctx] = loss_tile
    slope_sum = 2.0 * (mix_ratio * square_guided - cross)
    guided_coef = slope_sum * rescale_mix * sigma_cond / (cell_count * sigma_guided * sigma_guided * sigma_guided)
    guided_grad = mix_ratio * final_grad - guided_coef * (guided - sum_guided / cell_count)
    cond_coef = slope_sum * rescale_mix / (cell_count * sigma_guided * sigma_cond)
    cond_grad = (guidance * guided_grad + cond_coef * (cond_pred - sum_cond / cell_count)).astype(jnp.bfloat16)
    cond_rows = cond_grad.T

    def head_grad(cols):
        return dot_nn(cond_rows, hw_ref[:, cols]) * (1.0 + mod_ref[0, 1:2, cols])

    mean_one = row_mean(head_grad)
    mean_two = row_mean(lambda cols: head_grad(cols) * normed(cols))
    for cols in pieces:
        stream_grad = (head_grad(cols) - mean_one - normed(cols) * mean_two) * inverse
        p_buf[:, cols] = (gate_ref[:, cols] * stream_grad).astype(jnp.bfloat16)
        gs_ref[0, :, cols] = stream_grad.astype(jnp.bfloat16)

    side_x = place.x + 1 - 2 * (place.x % 2)
    side = place.z * 4 + side_x
    sibling = place.dp + 1 - 2 * place.core
    x_send, z_send = ag_send.at[0], ag_send.at[1]

    def beside(step):
        return ((place.z + step) % 4) * 4 + place.x

    def start(z_step, x):
        return slot_of((place.z + z_step) % 4, x, place.core) * tokens

    def part(z_step, x, cols, offset=0, count=None):
        return p_ref.at[pl.ds(pl.multiple_of(start(z_step, x) + offset, half), count or tokens), cols]

    def hand(ref, send, recv, dp, ctx):
        remote(ref, ref, send, recv, dp, ctx).start()

    def to_neighbours(ref, send, recv):
        hand(ref, send, recv.at[3], place.dp, beside(1))
        hand(ref, send, recv.at[1], place.dp, beside(3))

    def relay(x, cols, send, recv):
        hand(part(3, x, cols, 0, half), send, recv, place.dp, beside(1))
        hand(part(1, x, cols, half, half), send, recv, place.dp, beside(3))

    def to_sibling(ref, send, z_step):
        hand(ref, send, sib_recv.at[z_step], sibling, place.ctx)

    own = p_ref.at[pl.ds(pl.multiple_of(start(0, place.x), tokens), tokens), :]

    @pl.when(place.away == 0)
    def _():
        pltpu.make_async_copy(p_buf, own, p_recv).start()

    @pl.when(place.away == 1)
    def _():
        land = p_ref.at[rows_of(place.ctx, tokens), :]
        remote(p_buf, land, p_send, p_recv, sibling, place.mirror).start()

    @pl.when(place.away == 0)
    def _():
        send_heads(v_arg, v_ref, 2)


    pair = w_ref.at[:, rows_of(place.y, 2 * chunk)]
    wait_bytes(pair, w_recv.at[0])
    for step in range(1, 4):
        other = ((place.y + step) % 4) * 2 + place.core
        remote(pair, pair, w_send.at[2], w_recv.at[1], other, place.ctx).start()

    wait_bytes(own, p_recv)
    hand(part(0, place.x, x_cols), x_send, side_recv, place.dp, side)
    to_neighbours(part(0, place.x, z_cols), z_send, near_z_recv)
    to_neighbours(part(0, place.x, x_cols), x_send, own_x_recv)
    hand(part(0, place.x, z_cols), z_send, side_z_recv.at[0], place.dp, side)
    hand(own, own_send, sib_recv.at[0], sibling, place.ctx)
    share(mine_loss, losses, l_send, l_recv)

    @pl.when(place.away == 1)
    def _():
        wait_bytes(p_buf, p_send)
        send_heads(k_arg, k_ref, 1)
        send_heads(v_arg, v_ref, 2)


    def rows_at(z_step, which):
        return rows_of(((place.z + z_step) % 4) * 2 + which, tile)

    def forward(rows, keep):
        outs = []
        for head in range(2):
            cols = slice(head * HD, (head + 1) * HD)
            scores = dot_nt(q_ref[rows, cols], k_ref[:, cols])
            top = jnp.max(scores, axis=-1, keepdims=True)
            weights = jnp.exp2((scores - top) * EXP2_SCALE).astype(jnp.bfloat16)
            kept[keep, head] = weights
            sums = dot_nn(weights, v_ones[head])
            inverse = 1.0 / sums[:, HD:]
            out = sums[:, :HD] * inverse
            kept_out[keep, head] = out
            kept_inverse[keep, head] = inverse
            outs.append(out.astype(jnp.bfloat16))
        turned[:, rows] = jnp.concatenate(outs, axis=1).T

    def backward_head(rows, keep, head, out_grad):
        cols = slice(head * HD, (head + 1) * HD)
        q = q_ref[rows, cols]
        grad = (out_grad * kept_inverse[keep, head]).astype(jnp.bfloat16)
        delta = jnp.sum(grad.astype(jnp.float32) * kept_out[keep, head], axis=-1, keepdims=True)
        prob_grad = dot_nt(grad, v_ref[:, cols]) - delta
        weights = kept[keep, head]
        score_grad = (weights.astype(jnp.float32) * prob_grad).astype(jnp.bfloat16)
        dk_sum[head] += dot_nn(q.T, score_grad)
        dv_sum[head] += dot_nn(grad.T, weights)
        q_ref[rows, cols] = (dot_nn(score_grad, k_ref[:, cols]) * SCALE).astype(jnp.bfloat16)

    def backward(rows, keep):
        out_grad = dot_nt(p_ref[rows, :], w_ref[...])
        for head in range(2):
            backward_head(rows, keep, head, out_grad[:, head * HD : (head + 1) * HD])

    for near in (1, 3):
        wait_bytes(part(near, place.x, z_cols), near_z_recv.at[near])
    hand(part(1, place.x, z_cols), z_send, side_z_recv.at[1], place.dp, side)
    for near in (1, 3):
        to_sibling(part(near, place.x, z_cols), z_send, near)
    wait_bytes(part(0, side_x, x_cols), side_recv)
    to_neighbours(part(0, side_x, x_cols), x_send, side_x_recv)
    to_sibling(part(0, side_x, x_cols), x_send, 0)

    wait_bytes(part(0, side_x, z_cols), side_z_recv.at[0])
    hand(part(3, place.x, z_cols), z_send, side_z_recv.at[3], place.dp, side)
    relay(place.x, z_cols, z_send, far_z_recv)
    to_sibling(part(0, side_x, z_cols), z_send, 0)
    for near in (1, 3):
        wait_bytes(part(near, place.x, x_cols), own_x_recv.at[near])
    for near in (1, 3):
        to_sibling(part(near, place.x, x_cols), x_send, near)

    dk_sum[...] = jnp.zeros_like(dk_sum)
    dv_sum[...] = jnp.zeros_like(dv_sum)
    for index, ref in enumerate((q_ref, k_ref, v_ref)):
        wait_bytes(ref, a2a_recv.at[index])
    for head in range(2):
        v_ones[head, :, 0:HD] = v_ref[:, head * HD : (head + 1) * HD]
        v_ones[head, :, HD : 2 * HD] = jnp.ones((seq, HD), jnp.bfloat16)

    @pl.loop(0, 2)
    def _(which):
        forward(rows_at(2, which), which)

    wait_bytes(w_ref.at[:, pl.ds(0, 6 * chunk)], w_recv.at[1])

    @pl.loop(0, 6)
    def _(step):
        turn = step // 2
        z_step = turn + turn // 2

        @pl.when(step == 2)
        def _():
            wait_bytes(part(2, place.x, z_cols), far_z_recv)
            relay(place.x, x_cols, x_send, far_x_recv.at[0])
            hand(part(2, place.x, z_cols), z_send, side_z_recv.at[2], place.dp, side)
            to_sibling(part(2, place.x, z_cols), z_send, 2)
            wait_bytes(part(1, side_x, z_cols), side_z_recv.at[1])
            to_sibling(part(1, side_x, z_cols), z_send, 1)
            for near in (1, 3):
                wait_bytes(part(near, side_x, x_cols), side_x_recv.at[near])
            relay(side_x, x_cols, x_send, far_x_recv.at[1])
            for near in (1, 3):
                to_sibling(part(near, side_x, x_cols), x_send, near)

        @pl.when(step == 4)
        def _():
            wait_bytes(part(3, side_x, z_cols), side_z_recv.at[3])
            to_sibling(part(3, side_x, z_cols), z_send, 3)

        @pl.when(step % 2 == 1)
        def _():
            wait_bytes(p_ref.at[pl.ds(0, tile), :], sib_recv.at[z_step])

        rows = rows_at(z_step, (place.core + step) % 2)
        forward(rows, 2)
        backward(rows, 2)

    for far, x in ((0, place.x), (1, side_x)):
        wait_bytes(part(2, x, x_cols), far_x_recv.at[far])
        to_sibling(part(2, x, x_cols), x_send, 2)
    wait_bytes(part(2, side_x, z_cols), side_z_recv.at[2])
    to_sibling(part(2, side_x, z_cols), z_send, 2)

    def send_rows(src, dst_ref, shard, index, start=0, count=PAIR):
        own_shard = jnp.logical_and(place.away == 0, shard == place.ctx)
        rows = src.at[rows_of(shard, tokens), pl.ds(start, count)]
        land = dst_ref.at[0, :, pl.ds(pl.multiple_of(place.slot * PAIR + start, HD), count)]

        @pl.when(own_shard)
        def _():
            pltpu.make_async_copy(rows, land, out_recv.at[index]).start()

        @pl.when(jnp.logical_not(own_shard))
        def _():
            remote(rows, land, out_send.at[index], out_recv.at[index], user, shard).start()

    @pl.loop(0, 12)
    def _(step):
        turn = step // 4
        send_rows(q_ref, gq_ref, ((place.z + turn + turn // 2) % 4) * 4 + (step + place.x) % 4, 0)

    wait_bytes(p_ref.at[pl.ds(0, tile), :], sib_recv.at[2])

    wide = width // 4

    def proj_part(y):
        return dot_nn(turned[...], p_ref[:, rows_of(y, wide)]).astype(jnp.bfloat16)

    @pl.loop(0, 3)
    def _(step):
        y = (place.y + 2 + step + step // 2) % 4
        g_out[y] = proj_part(y)
        remote(g_out.at[y], g_in.at[place.y], g_send, g_recv, y * 2 + place.core, place.ctx).start()

    @pl.loop(0, 2)
    def _(which):
        last_grad[which] = dot_nt(p_ref[rows_at(2, which), :], w_ref[...])

    for head in range(2):
        cols = slice(head * HD, (head + 1) * HD)

        @pl.loop(0, 2)
        def _(which):
            backward_head(rows_at(2, which), which, head, last_grad[which, :, cols])

        k_ref[:, cols] = (dk_sum[head] * SCALE).astype(jnp.bfloat16).T
        v_ref[:, cols] = dv_sum[head].astype(jnp.bfloat16).T

        @pl.loop(0, SHARDS)
        def _(step):
            shard = (place.ctx + step) % SHARDS
            send_rows(k_ref, gk_ref, shard, 1, head * HD, HD)
            send_rows(v_ref, gv_ref, shard, 2, head * HD, HD)

    @pl.loop(0, 4)
    def _(step):
        send_rows(q_ref, gq_ref, ((place.z + 2) % 4) * 4 + (step + place.x) % 4, 0)

    g_in[place.y] = proj_part(place.y)
    settle(losses, l_send, l_recv)
    loss_ref[...] = jnp.sum(losses[...], axis=0) / cell_count

    wait_bytes(g_in.at[pl.ds(0, 3)], g_recv)
    total_g = jnp.sum(g_in[...].astype(jnp.float32), axis=0)
    g_pair[0] = total_g[:, : wide // 2].astype(jnp.bfloat16)
    g_pair[1] = total_g[:, wide // 2 :].astype(jnp.bfloat16)

    @pl.when(place.away == 0)
    def _():
        remote(g_pair.at[1 - place.core], g_last.at[0], h_send.at[0], h_recv.at[0], sibling, place.ctx).start()
        g_last[0] = g_pair[place.core]

    @pl.when(place.away == 1)
    def _():
        for core in range(2):
            remote(
                g_pair.at[core], g_last.at[1], h_send.at[core], h_recv.at[1], place.y * 2 + core, place.mirror
            ).start()
        wait_bytes(g_last.at[0], h_recv.at[0])

    wait_bytes(g_last.at[1], h_recv.at[1])
    gp_ref[...] = g_last[0].astype(jnp.float32) + g_last[1].astype(jnp.float32)

    for index, ref in enumerate((gq_ref, gk_ref, gv_ref)):
        wait_bytes(ref, out_recv.at[index])

    @pl.loop(0, SHARDS - 1 + place.away)
    def _(step):
        for index in range(3):
            wait_bytes(q_ref.at[pl.ds(0, tokens), :], a2a_send.at[index])
            wait_bytes(q_ref.at[pl.ds(0, tokens), :], out_send.at[index])

    wait_bytes(g_pair.at[0], h_send.at[0])
    wait_bytes(g_out.at[pl.ds(0, 3)], g_send)
    wait_bytes(w_ref.at[:, pl.ds(0, chunk)], w_send.at[1])
    wait_bytes(w_ref.at[:, pl.ds(0, 6 * chunk)], w_send.at[2])

    @pl.when(place.away == 1)
    def _():
        wait_bytes(g_pair.at[1], h_send.at[1])
        wait_bytes(w_ref.at[:, pl.ds(0, chunk)], w_send.at[0])

    wait_bytes(p_buf, own_send)
    wait_bytes(p_ref.at[pl.ds(0, 14 * tokens), x_cols], x_send)
    wait_bytes(p_ref.at[pl.ds(0, 14 * tokens), z_cols], z_send)


def hand_over(*refs):
    sources, loss, results, loss_out = refs[:5], refs[5], refs[6:11], refs[11]
    held, arrived, left = refs[12:17], refs[17], refs[18]
    fetches = [pltpu.make_async_copy(sources[i], held[i], arrived.at[i]) for i in range(5)]
    stores = [pltpu.make_async_copy(held[i], results[i], left.at[i]) for i in range(5)]
    for fetch in fetches:
        fetch.start()
    loss_out[0] = loss[0, 0]
    for fetch, store in zip(fetches, stores):
        fetch.wait()
        store.start()
    for store in stores:
        store.wait()


def per_device(
    query, key_states, value_states, block_out, gate_mod, head_mod, head_weight, proj_weight, uncond_pred, target
):
    tokens, features = query.shape[1:]
    seq = tokens * SHARDS
    width = block_out.shape[2]
    vmem = pl.BlockSpec(memory_space=pltpu.VMEM)
    hbm = pl.BlockSpec(memory_space=pl.ANY)
    grad = jax.ShapeDtypeStruct(query.shape, jnp.bfloat16)
    dma = pltpu.SemaphoreType.DMA
    low, wide = jnp.bfloat16, jnp.float32
    grads = pl.pallas_call(
        kernel,
        out_shape=[
            grad, grad, grad,
            jax.ShapeDtypeStruct(block_out.shape, low),
            jax.ShapeDtypeStruct(proj_weight.shape, wide),
            jax.ShapeDtypeStruct((8, 128), wide),
        ],
        in_specs=[hbm] * 3 + [vmem] * 7,
        out_specs=[hbm] * 3 + [vmem] * 3,
        scratch_shapes=[
            pltpu.VMEM((seq, PAIR), low),
            pltpu.VMEM((seq, PAIR), low),
            pltpu.VMEM((seq, PAIR), low),
            pltpu.VMEM((PAIR, width), low),
            pltpu.VMEM((seq, width), low),
            pltpu.VMEM((tokens, width), low),
            pltpu.VMEM((SHARDS, 8, 128), wide),
            pltpu.VMEM((SHARDS, 8, 128), wide),
            pltpu.VMEM((8, 128), wide),
            pltpu.VMEM((8, 128), wide),
            pltpu.VMEM((2, seq, PAIR), low),
            pltpu.VMEM((2, 2 * tokens, PAIR), wide),
            pltpu.VMEM((3, 2, 2 * tokens, seq), low),
            pltpu.VMEM((3, 2, 2 * tokens, HD), wide),
            pltpu.VMEM((3, 2, 2 * tokens, HD), wide),
            pltpu.VMEM((2, HD, seq), wide),
            pltpu.VMEM((2, HD, seq), wide),
            pltpu.VMEM((PAIR, seq), low),
            pltpu.VMEM((4, PAIR, width // 4), low),
            pltpu.VMEM((4, PAIR, width // 4), low),
            pltpu.VMEM((2, PAIR, width // 8), low),
            pltpu.VMEM((2, PAIR, width // 8), low),
            dma((3,)), dma((3,)), dma((3,)), dma((2,)),
            dma, dma, dma, dma, dma, dma,
            dma((2,)), dma, dma, dma((4,)), dma((4,)), dma((2,)), dma((4,)), dma, dma((4,)), dma((4,)),
            dma((3,)), dma((3,)), dma, dma, dma((2,)), dma((2,)),
        ],
        compiler_params=pltpu.CompilerParams(
            collective_id=0, has_side_effects=True, vmem_limit_bytes=63 * 2**20
        ),
    )(
        query, key_states, value_states, block_out, gate_mod, head_mod, head_weight, proj_weight,
        jnp.swapaxes(uncond_pred, 1, 2), jnp.swapaxes(target, 1, 2),
    )
    smem = pl.BlockSpec(memory_space=pltpu.SMEM)
    return pl.pallas_call(
        hand_over,
        out_shape=[jax.ShapeDtypeStruct(array.shape, array.dtype) for array in grads[:5]]
        + [jax.ShapeDtypeStruct((1,), wide)],
        in_specs=[hbm] * 5 + [smem],
        out_specs=[hbm] * 5 + [smem],
        scratch_shapes=[pltpu.VMEM(array.shape, array.dtype) for array in grads[:5]] + [dma((5,)), dma((5,))],
        compiler_params=pltpu.CompilerParams(vmem_limit_bytes=63 * 2**20),
    )(*grads)


def solution(mesh):
    return jax.shard_map(
        per_device,
        mesh=mesh,
        in_specs=(
            P("dp", "ctx", None),
            P("dp", "ctx", None),
            P("dp", "ctx", None),
            P("dp", "ctx", None),
            P("dp", None),
            P("dp", None, None),
            P(),
            P("ctx", "dp"),
            P("dp", "ctx", None),
            P("dp", "ctx", None),
        ),
        out_specs=(
            P("dp", "ctx", None),
            P("dp", "ctx", None),
            P("dp", "ctx", None),
            P("dp", "ctx", None),
            P("ctx", "dp"),
            P("dp"),
        ),
        check_vma=False,
    )
```

```python
import functools

import jax
import jax.numpy as jnp
from jax import lax
from jax.experimental import pallas as pl
from jax.experimental.pallas import tpu as pltpu
from jax.sharding import PartitionSpec as P

HD = 128
PAIR = 2 * HD
SHARDS = 16
SCALE = 1.0 / float(HD) ** 0.5
EXP2_SCALE = 1.4426950408889634 * SCALE
MESH = pl.DeviceIdType.MESH

guidance = 5.0
rescale_mix = 0.7
norm_epsilon = 1e-06
spread_epsilon = 1e-05


def dot_nt(left, right):
    return lax.dot_general(left, right, (((1,), (1,)), ((), ())), preferred_element_type=jnp.float32)


def dot_nn(left, right):
    return lax.dot_general(left, right, (((1,), (0,)), ((), ())), preferred_element_type=jnp.float32)


def sigma_of(first_sum, square_sum, cell_count):
    mean_value = first_sum / cell_count
    return jnp.sqrt(square_sum / cell_count - mean_value * mean_value + spread_epsilon)


class Place:
    def __init__(self):
        dp = lax.axis_index("dp")
        ctx = lax.axis_index("ctx")
        self.dp, self.ctx = dp, ctx
        self.y, self.core = dp // 2, dp % 2
        self.z, self.x = ctx // 4, ctx % 4
        self.half = self.x // 2
        self.away = (self.core + self.half) % 2
        self.slot = self.z * 4 + self.x + self.away * (3 - 2 * self.x)
        self.mirror = self.z * 4 + 3 - self.x


def slot_of(z, x, core):
    away = (core + x // 2) % 2
    return z * 4 + x + away * (3 - 2 * x)


def greet(place):
    barrier = pltpu.get_barrier_semaphore()

    @pl.loop(0, 2 * SHARDS)
    def _(index):
        core, ctx = index // SHARDS, index % SHARDS
        own = jnp.logical_and(core == place.core, ctx == place.ctx)

        @pl.when(jnp.logical_not(own))
        def _():
            pl.semaphore_signal(
                barrier, inc=1, device_id=(place.y * 2 + core, ctx), device_id_type=MESH
            )

    for step in range(1, 4):
        other = ((place.y + step) % 4) * 2 + place.core
        pl.semaphore_signal(barrier, inc=1, device_id=(other, place.ctx), device_id_type=MESH)
    pl.semaphore_wait(barrier, 2 * SHARDS - 1 + 3)


def remote(src, dst, send_sem, recv_sem, dp, ctx):
    return pltpu.make_async_remote_copy(
        src_ref=src, dst_ref=dst, send_sem=send_sem, recv_sem=recv_sem, device_id=(dp, ctx), device_id_type=MESH
    )


def wait_bytes(ref, sem):
    pltpu.make_async_copy(ref, ref, sem).wait()


def rows_of(index, count):
    return pl.ds(pl.multiple_of(index * count, count), count)


def kernel(
    q_arg, k_arg, v_arg, stream_ref, gate_ref, mod_ref, hw_ref, pw_ref, uncond_ref, target_ref,
    gq_ref, gk_ref, gv_ref, gs_ref, gp_ref, loss_ref,
    q_ref, k_ref, v_ref, w_ref, p_ref, p_buf, moments, losses, mine, mine_loss,
    v_ones, last_grad, kept, kept_out, kept_inverse, dk_sum, dv_sum, turned, g_out, g_in, g_pair, g_last,
    a2a_send, a2a_recv, w_send, w_recv, m_send, m_recv, l_send, l_recv, p_send, p_recv,
    ag_send, own_send, side_recv, own_x_recv, side_x_recv, far_x_recv, near_z_recv, far_z_recv, side_z_recv, sib_recv,
    out_send, out_recv, g_send, g_recv, h_send, h_recv,
):
    place = Place()
    tokens = stream_ref.shape[1]
    seq, width = p_ref.shape
    chunk = pw_ref.shape[1]
    cell_count = float(seq * uncond_ref.shape[1])
    half = tokens // 2
    tile = 2 * tokens
    first_cols = (width // 128 * 28 // 40) * 128
    x_cols, z_cols = pl.ds(0, first_cols), pl.ds(first_cols, width - first_cols)
    greet(place)

    def send_heads(src, dst, index):
        @pl.loop(0, SHARDS)
        def _(step):
            z = (place.z + step // 4) % 4
            x = 2 * place.core + (step // 2 + place.x) % 2
            core = (step + place.core) % 2
            slot = slot_of(z, x, core)
            own = jnp.logical_and(core == place.core, z * 4 + x == place.ctx)
            part = src.at[0, :, rows_of(slot, PAIR)]
            land = dst.at[rows_of(place.ctx, tokens), :]

            @pl.when(own)
            def _():
                pltpu.make_async_copy(part, land, a2a_recv.at[index]).start()

            @pl.when(jnp.logical_not(own))
            def _():
                remote(part, land, a2a_send.at[index], a2a_recv.at[index], place.y * 2 + core, z * 4 + x).start()

    own_cols = w_ref.at[:, rows_of(place.dp, chunk)]
    user = place.y * 2 + place.half

    @pl.when(place.away == 0)
    def _():
        pltpu.make_async_copy(pw_ref, own_cols, w_recv.at[0]).start()

    @pl.when(place.away == 1)
    def _():
        remote(pw_ref, own_cols, w_send.at[0], w_recv.at[0], user, place.ctx).start()


    @pl.when(place.away == 0)
    def _():
        send_heads(q_arg, q_ref, 0)


    step_cols = PAIR
    pieces = [slice(start, start + step_cols) for start in range(0, width, step_cols)]

    def values(cols):
        return stream_ref[0, :, cols].astype(jnp.float32)

    def row_mean(term):
        folded = jnp.zeros((tokens, HD), jnp.float32)
        for cols in pieces:
            piece = term(cols)
            folded += piece[:, :HD] + piece[:, HD:]
        return jnp.sum(folded, axis=-1, keepdims=True) / width

    center = row_mean(values)
    inverse = lax.rsqrt(row_mean(lambda cols: jnp.square(values(cols) - center)) + norm_epsilon)

    def normed(cols):
        return (values(cols) - center) * inverse

    for cols in pieces:
        hidden = normed(cols) * (1.0 + mod_ref[0, 1:2, cols]) + mod_ref[0, 0:1, cols]
        p_buf[:, cols] = hidden.astype(jnp.bfloat16)
    cond_pred = dot_nt(p_buf[...], hw_ref[...]).T
    uncond = uncond_ref[0]
    target = target_ref[0]
    guided = uncond + guidance * (cond_pred - uncond)

    def total(array):
        return jnp.sum(jnp.sum(array, axis=0, keepdims=True), axis=1, keepdims=True)

    lane = lax.broadcasted_iota(jnp.int32, (8, 128), 1)
    tally = jnp.zeros((8, 128), jnp.float32)
    for index, array in enumerate(
        (cond_pred, cond_pred * cond_pred, guided, guided * guided, guided * target)
    ):
        tally = jnp.where(lane == index, total(array), tally)
    mine[...] = tally

    def share(src, dst, send, recv):
        @pl.loop(1, SHARDS)
        def _(step):
            ctx = (place.ctx + step) % SHARDS
            remote(src, dst.at[place.ctx], send, recv, place.dp, ctx).start()

    def settle(dst, send, recv):
        wait_bytes(dst.at[pl.ds(0, SHARDS - 1)], recv)
        wait_bytes(dst.at[pl.ds(0, SHARDS - 1)], send)

    moments[place.ctx] = tally
    share(mine, moments, m_send, m_recv)

    @pl.when(place.away == 0)
    def _():
        send_heads(k_arg, k_ref, 1)


    settle(moments, m_send, m_recv)
    sums = jnp.sum(moments[...], axis=0)
    sum_cond, square_cond, sum_guided, square_guided, cross = [sums[0:1, i : i + 1] for i in range(5)]
    sigma_cond = sigma_of(sum_cond, square_cond, cell_count)
    sigma_guided = sigma_of(sum_guided, square_guided, cell_count)
    mix_ratio = rescale_mix * sigma_cond / sigma_guided + (1.0 - rescale_mix)
    final = mix_ratio * guided
    final_grad = 2.0 * (final - target)
    loss_tile = jnp.broadcast_to(total(jnp.square(final - target)), (8, 128))
    mine_loss[...] = loss_tile
    losses[place.ctx] = loss_tile
    slope_sum = 2.0 * (mix_ratio * square_guided - cross)
    guided_coef = slope_sum * rescale_mix * sigma_cond / (cell_count * sigma_guided * sigma_guided * sigma_guided)
    guided_grad = mix_ratio * final_grad - guided_coef * (guided - sum_guided / cell_count)
    cond_coef = slope_sum * rescale_mix / (cell_count * sigma_guided * sigma_cond)
    cond_grad = (guidance * guided_grad + cond_coef * (cond_pred - sum_cond / cell_count)).astype(jnp.bfloat16)
    cond_rows = cond_grad.T

    def head_grad(cols):
        return dot_nn(cond_rows, hw_ref[:, cols]) * (1.0 + mod_ref[0, 1:2, cols])

    mean_one = row_mean(head_grad)
    mean_two = row_mean(lambda cols: head_grad(cols) * normed(cols))
    for cols in pieces:
        stream_grad = (head_grad(cols) - mean_one - normed(cols) * mean_two) * inverse
        p_buf[:, cols] = (gate_ref[:, cols] * stream_grad).astype(jnp.bfloat16)
        gs_ref[0, :, cols] = stream_grad.astype(jnp.bfloat16)

    side_x = place.x + 1 - 2 * (place.x % 2)
    side = place.z * 4 + side_x
    sibling = place.dp + 1 - 2 * place.core
    x_send, z_send = ag_send.at[0], ag_send.at[1]

    def beside(step):
        return ((place.z + step) % 4) * 4 + place.x

    def start(z_step, x):
        return slot_of((place.z + z_step) % 4, x, place.core) * tokens

    def part(z_step, x, cols, offset=0, count=None):
        return p_ref.at[pl.ds(pl.multiple_of(start(z_step, x) + offset, half), count or tokens), cols]

    def hand(ref, send, recv, dp, ctx):
        remote(ref, ref, send, recv, dp, ctx).start()

    def to_neighbours(ref, send, recv):
        hand(ref, send, recv.at[3], place.dp, beside(1))
        hand(ref, send, recv.at[1], place.dp, beside(3))

    def relay(x, cols, send, recv):
        hand(part(3, x, cols, 0, half), send, recv, place.dp, beside(1))
        hand(part(1, x, cols, half, half), send, recv, place.dp, beside(3))

    def to_sibling(ref, send, z_step):
        hand(ref, send, sib_recv.at[z_step], sibling, place.ctx)

    own = p_ref.at[pl.ds(pl.multiple_of(start(0, place.x), tokens), tokens), :]

    @pl.when(place.away == 0)
    def _():
        pltpu.make_async_copy(p_buf, own, p_recv).start()

    @pl.when(place.away == 1)
    def _():
        land = p_ref.at[rows_of(place.ctx, tokens), :]
        remote(p_buf, land, p_send, p_recv, sibling, place.mirror).start()

    @pl.when(place.away == 0)
    def _():
        send_heads(v_arg, v_ref, 2)


    wait_bytes(own, p_recv)
    hand(part(0, place.x, x_cols), x_send, side_recv, place.dp, side)
    to_neighbours(part(0, place.x, z_cols), z_send, near_z_recv)
    to_neighbours(part(0, place.x, x_cols), x_send, own_x_recv)
    hand(part(0, place.x, z_cols), z_send, side_z_recv.at[0], place.dp, side)
    hand(own, own_send, sib_recv.at[0], sibling, place.ctx)
    share(mine_loss, losses, l_send, l_recv)

    @pl.when(place.away == 1)
    def _():
        wait_bytes(p_buf, p_send)
        send_heads(q_arg, q_ref, 0)
        send_heads(k_arg, k_ref, 1)
        send_heads(v_arg, v_ref, 2)


    remote(pw_ref, own_cols, w_send.at[1], w_recv.at[0], user, place.mirror).start()

    pair = w_ref.at[:, rows_of(place.y, 2 * chunk)]
    wait_bytes(pair, w_recv.at[0])
    for step in range(1, 4):
        other = ((place.y + step) % 4) * 2 + place.core
        remote(pair, pair, w_send.at[2], w_recv.at[1], other, place.ctx).start()

    def rows_at(z_step, which):
        return rows_of(((place.z + z_step) % 4) * 2 + which, tile)

    def forward(rows, keep):
        outs = []
        for head in range(2):
            cols = slice(head * HD, (head + 1) * HD)
            scores = dot_nt(q_ref[rows, cols], k_ref[:, cols])
            top = jnp.max(scores, axis=-1, keepdims=True)
            weights = jnp.exp2((scores - top) * EXP2_SCALE).astype(jnp.bfloat16)
            kept[keep, head] = weights
            sums = dot_nn(weights, v_ones[head])
            inverse = 1.0 / sums[:, HD:]
            out = sums[:, :HD] * inverse
            kept_out[keep, head] = out
            kept_inverse[keep, head] = inverse
            outs.append(out.astype(jnp.bfloat16))
        turned[:, rows] = jnp.concatenate(outs, axis=1).T

    def backward_head(rows, keep, head, out_grad):
        cols = slice(head * HD, (head + 1) * HD)
        q = q_ref[rows, cols]
        grad = (out_grad * kept_inverse[keep, head]).astype(jnp.bfloat16)
        delta = jnp.sum(grad.astype(jnp.float32) * kept_out[keep, head], axis=-1, keepdims=True)
        prob_grad = dot_nt(grad, v_ref[:, cols]) - delta
        weights = kept[keep, head]
        score_grad = (weights.astype(jnp.float32) * prob_grad).astype(jnp.bfloat16)
        dk_sum[head] += dot_nn(q.T, score_grad)
        dv_sum[head] += dot_nn(grad.T, weights)
        q_ref[rows, cols] = (dot_nn(score_grad, k_ref[:, cols]) * SCALE).astype(jnp.bfloat16)

    def backward(rows, keep):
        out_grad = dot_nt(p_ref[rows, :], w_ref[...])
        for head in range(2):
            backward_head(rows, keep, head, out_grad[:, head * HD : (head + 1) * HD])

    for near in (1, 3):
        wait_bytes(part(near, place.x, z_cols), near_z_recv.at[near])
    hand(part(1, place.x, z_cols), z_send, side_z_recv.at[1], place.dp, side)
    for near in (1, 3):
        to_sibling(part(near, place.x, z_cols), z_send, near)
    wait_bytes(part(0, side_x, x_cols), side_recv)
    to_neighbours(part(0, side_x, x_cols), x_send, side_x_recv)
    to_sibling(part(0, side_x, x_cols), x_send, 0)

    wait_bytes(part(0, side_x, z_cols), side_z_recv.at[0])
    hand(part(3, place.x, z_cols), z_send, side_z_recv.at[3], place.dp, side)
    relay(place.x, z_cols, z_send, far_z_recv)
    to_sibling(part(0, side_x, z_cols), z_send, 0)
    for near in (1, 3):
        wait_bytes(part(near, place.x, x_cols), own_x_recv.at[near])
    for near in (1, 3):
        to_sibling(part(near, place.x, x_cols), x_send, near)

    dk_sum[...] = jnp.zeros_like(dk_sum)
    dv_sum[...] = jnp.zeros_like(dv_sum)
    for index, ref in enumerate((q_ref, k_ref, v_ref)):
        wait_bytes(ref, a2a_recv.at[index])
    for head in range(2):
        v_ones[head, :, 0:HD] = v_ref[:, head * HD : (head + 1) * HD]
        v_ones[head, :, HD : 2 * HD] = jnp.ones((seq, HD), jnp.bfloat16)

    @pl.loop(0, 2)
    def _(which):
        forward(rows_at(2, which), which)

    wait_bytes(w_ref.at[:, pl.ds(0, 6 * chunk)], w_recv.at[1])

    @pl.loop(0, 6)
    def _(step):
        turn = step // 2
        z_step = turn + turn // 2

        @pl.when(step == 2)
        def _():
            wait_bytes(part(2, place.x, z_cols), far_z_recv)
            relay(place.x, x_cols, x_send, far_x_recv.at[0])
            hand(part(2, place.x, z_cols), z_send, side_z_recv.at[2], place.dp, side)
            to_sibling(part(2, place.x, z_cols), z_send, 2)
            wait_bytes(part(1, side_x, z_cols), side_z_recv.at[1])
            to_sibling(part(1, side_x, z_cols), z_send, 1)
            for near in (1, 3):
                wait_bytes(part(near, side_x, x_cols), side_x_recv.at[near])
            relay(side_x, x_cols, x_send, far_x_recv.at[1])
            for near in (1, 3):
                to_sibling(part(near, side_x, x_cols), x_send, near)

        @pl.when(step == 4)
        def _():
            wait_bytes(part(3, side_x, z_cols), side_z_recv.at[3])
            to_sibling(part(3, side_x, z_cols), z_send, 3)

        @pl.when(step % 2 == 1)
        def _():
            wait_bytes(p_ref.at[pl.ds(0, tile), :], sib_recv.at[z_step])

        rows = rows_at(z_step, (place.core + step) % 2)
        forward(rows, 2)
        backward(rows, 2)

    for far, x in ((0, place.x), (1, side_x)):
        wait_bytes(part(2, x, x_cols), far_x_recv.at[far])
        to_sibling(part(2, x, x_cols), x_send, 2)
    wait_bytes(part(2, side_x, z_cols), side_z_recv.at[2])
    to_sibling(part(2, side_x, z_cols), z_send, 2)

    def send_rows(src, dst_ref, shard, index, start=0, count=PAIR):
        own_shard = jnp.logical_and(place.away == 0, shard == place.ctx)
        rows = src.at[rows_of(shard, tokens), pl.ds(start, count)]
        land = dst_ref.at[0, :, pl.ds(pl.multiple_of(place.slot * PAIR + start, HD), count)]

        @pl.when(own_shard)
        def _():
            pltpu.make_async_copy(rows, land, out_recv.at[index]).start()

        @pl.when(jnp.logical_not(own_shard))
        def _():
            remote(rows, land, out_send.at[index], out_recv.at[index], user, shard).start()

    @pl.loop(0, 12)
    def _(step):
        turn = step // 4
        send_rows(q_ref, gq_ref, ((place.z + turn + turn // 2) % 4) * 4 + (step + place.x) % 4, 0)

    wait_bytes(p_ref.at[pl.ds(0, tile), :], sib_recv.at[2])

    wide = width // 4

    def proj_part(y):
        return dot_nn(turned[...], p_ref[:, rows_of(y, wide)]).astype(jnp.bfloat16)

    @pl.loop(0, 3)
    def _(step):
        y = (place.y + 2 + step + step // 2) % 4
        g_out[y] = proj_part(y)
        remote(g_out.at[y], g_in.at[place.y], g_send, g_recv, y * 2 + place.core, place.ctx).start()

    @pl.loop(0, 2)
    def _(which):
        last_grad[which] = dot_nt(p_ref[rows_at(2, which), :], w_ref[...])

    for head in range(2):
        cols = slice(head * HD, (head + 1) * HD)

        @pl.loop(0, 2)
        def _(which):
            backward_head(rows_at(2, which), which, head, last_grad[which, :, cols])

        k_ref[:, cols] = (dk_sum[head] * SCALE).astype(jnp.bfloat16).T
        v_ref[:, cols] = dv_sum[head].astype(jnp.bfloat16).T

        @pl.loop(0, SHARDS)
        def _(step):
            shard = (place.ctx + step) % SHARDS
            send_rows(k_ref, gk_ref, shard, 1, head * HD, HD)
            send_rows(v_ref, gv_ref, shard, 2, head * HD, HD)

    @pl.loop(0, 4)
    def _(step):
        send_rows(q_ref, gq_ref, ((place.z + 2) % 4) * 4 + (step + place.x) % 4, 0)

    g_in[place.y] = proj_part(place.y)
    settle(losses, l_send, l_recv)
    loss_ref[...] = jnp.sum(losses[...], axis=0) / cell_count

    wait_bytes(g_in.at[pl.ds(0, 3)], g_recv)
    total_g = jnp.sum(g_in[...].astype(jnp.float32), axis=0)
    g_pair[0] = total_g[:, : wide // 2].astype(jnp.bfloat16)
    g_pair[1] = total_g[:, wide // 2 :].astype(jnp.bfloat16)

    @pl.when(place.away == 0)
    def _():
        remote(g_pair.at[1 - place.core], g_last.at[0], h_send.at[0], h_recv.at[0], sibling, place.ctx).start()
        g_last[0] = g_pair[place.core]

    @pl.when(place.away == 1)
    def _():
        for core in range(2):
            remote(
                g_pair.at[core], g_last.at[1], h_send.at[core], h_recv.at[1], place.y * 2 + core, place.mirror
            ).start()
        wait_bytes(g_last.at[0], h_recv.at[0])

    wait_bytes(g_last.at[1], h_recv.at[1])
    gp_ref[...] = g_last[0].astype(jnp.float32) + g_last[1].astype(jnp.float32)

    for index, ref in enumerate((gq_ref, gk_ref, gv_ref)):
        wait_bytes(ref, out_recv.at[index])

    @pl.loop(0, SHARDS - 1 + place.away)
    def _(step):
        for index in range(3):
            wait_bytes(q_ref.at[pl.ds(0, tokens), :], a2a_send.at[index])
            wait_bytes(q_ref.at[pl.ds(0, tokens), :], out_send.at[index])

    wait_bytes(g_pair.at[0], h_send.at[0])
    wait_bytes(g_out.at[pl.ds(0, 3)], g_send)
    wait_bytes(w_ref.at[:, pl.ds(0, chunk)], w_send.at[1])
    wait_bytes(w_ref.at[:, pl.ds(0, 6 * chunk)], w_send.at[2])

    @pl.when(place.away == 1)
    def _():
        wait_bytes(g_pair.at[1], h_send.at[1])
        wait_bytes(w_ref.at[:, pl.ds(0, chunk)], w_send.at[0])

    wait_bytes(p_buf, own_send)
    wait_bytes(p_ref.at[pl.ds(0, 14 * tokens), x_cols], x_send)
    wait_bytes(p_ref.at[pl.ds(0, 14 * tokens), z_cols], z_send)


def hand_over(*refs):
    sources, loss, results, loss_out = refs[:5], refs[5], refs[6:11], refs[11]
    held, arrived, left = refs[12:17], refs[17], refs[18]
    fetches = [pltpu.make_async_copy(sources[i], held[i], arrived.at[i]) for i in range(5)]
    stores = [pltpu.make_async_copy(held[i], results[i], left.at[i]) for i in range(5)]
    for fetch in fetches:
        fetch.start()
    loss_out[0] = loss[0, 0]
    for fetch, store in zip(fetches, stores):
        fetch.wait()
        store.start()
    for store in stores:
        store.wait()


def per_device(
    query, key_states, value_states, block_out, gate_mod, head_mod, head_weight, proj_weight, uncond_pred, target
):
    tokens, features = query.shape[1:]
    seq = tokens * SHARDS
    width = block_out.shape[2]
    vmem = pl.BlockSpec(memory_space=pltpu.VMEM)
    hbm = pl.BlockSpec(memory_space=pl.ANY)
    grad = jax.ShapeDtypeStruct(query.shape, jnp.bfloat16)
    dma = pltpu.SemaphoreType.DMA
    low, wide = jnp.bfloat16, jnp.float32
    grads = pl.pallas_call(
        kernel,
        out_shape=[
            grad, grad, grad,
            jax.ShapeDtypeStruct(block_out.shape, low),
            jax.ShapeDtypeStruct(proj_weight.shape, wide),
            jax.ShapeDtypeStruct((8, 128), wide),
        ],
        in_specs=[hbm] * 3 + [vmem] * 7,
        out_specs=[hbm] * 3 + [vmem] * 3,
        scratch_shapes=[
            pltpu.VMEM((seq, PAIR), low),
            pltpu.VMEM((seq, PAIR), low),
            pltpu.VMEM((seq, PAIR), low),
            pltpu.VMEM((PAIR, width), low),
            pltpu.VMEM((seq, width), low),
            pltpu.VMEM((tokens, width), low),
            pltpu.VMEM((SHARDS, 8, 128), wide),
            pltpu.VMEM((SHARDS, 8, 128), wide),
            pltpu.VMEM((8, 128), wide),
            pltpu.VMEM((8, 128), wide),
            pltpu.VMEM((2, seq, PAIR), low),
            pltpu.VMEM((2, 2 * tokens, PAIR), wide),
            pltpu.VMEM((3, 2, 2 * tokens, seq), low),
            pltpu.VMEM((3, 2, 2 * tokens, HD), wide),
            pltpu.VMEM((3, 2, 2 * tokens, HD), wide),
            pltpu.VMEM((2, HD, seq), wide),
            pltpu.VMEM((2, HD, seq), wide),
            pltpu.VMEM((PAIR, seq), low),
            pltpu.VMEM((4, PAIR, width // 4), low),
            pltpu.VMEM((4, PAIR, width // 4), low),
            pltpu.VMEM((2, PAIR, width // 8), low),
            pltpu.VMEM((2, PAIR, width // 8), low),
            dma((3,)), dma((3,)), dma((3,)), dma((2,)),
            dma, dma, dma, dma, dma, dma,
            dma((2,)), dma, dma, dma((4,)), dma((4,)), dma((2,)), dma((4,)), dma, dma((4,)), dma((4,)),
            dma((3,)), dma((3,)), dma, dma, dma((2,)), dma((2,)),
        ],
        compiler_params=pltpu.CompilerParams(
            collective_id=0, has_side_effects=True, vmem_limit_bytes=63 * 2**20
        ),
    )(
        query, key_states, value_states, block_out, gate_mod, head_mod, head_weight, proj_weight,
        jnp.swapaxes(uncond_pred, 1, 2), jnp.swapaxes(target, 1, 2),
    )
    smem = pl.BlockSpec(memory_space=pltpu.SMEM)
    return pl.pallas_call(
        hand_over,
        out_shape=[jax.ShapeDtypeStruct(array.shape, array.dtype) for array in grads[:5]]
        + [jax.ShapeDtypeStruct((1,), wide)],
        in_specs=[hbm] * 5 + [smem],
        out_specs=[hbm] * 5 + [smem],
        scratch_shapes=[pltpu.VMEM(array.shape, array.dtype) for array in grads[:5]] + [dma((5,)), dma((5,))],
        compiler_params=pltpu.CompilerParams(vmem_limit_bytes=63 * 2**20),
    )(*grads)


def solution(mesh):
    return jax.shard_map(
        per_device,
        mesh=mesh,
        in_specs=(
            P("dp", "ctx", None),
            P("dp", "ctx", None),
            P("dp", "ctx", None),
            P("dp", "ctx", None),
            P("dp", None),
            P("dp", None, None),
            P(),
            P("ctx", "dp"),
            P("dp", "ctx", None),
            P("dp", "ctx", None),
        ),
        out_specs=(
            P("dp", "ctx", None),
            P("dp", "ctx", None),
            P("dp", "ctx", None),
            P("dp", "ctx", None),
            P("ctx", "dp"),
            P("dp"),
        ),
        check_vma=False,
    )
```
